32 devices in a mesh: groups: 2 (over y), tensor: 8 (over z, x), replica: 2 (over core).
Axes of the slice: x: 2, y: 2, z: 4, core: 2. Of those that a mesh axis runs over, the one named last changes fastest.
Arguments:
- hidden: bfloat16 [4, 28672, 128], P(('groups', 'replica'), 'tensor'), parts along dimension 0, may hold values from -6 to 6
- down_weight: bfloat16 [28672, 8192], P('tensor'), may hold values from -0.03125 to 0.03125
- residual: bfloat16 [4, 64, 128, 128], P(('groups', 'replica'), 'tensor'), parts along dimension 0, may hold values from -3 to 3
- norm_gain: float32 [8192], replicated, may hold values from 0.25 to 1.75
- query_weight: bfloat16 [8192, 8192], P('tensor'), may hold values from -0.0625 to 0.0625
- prefix_len: int32 [4], P(('groups', 'replica')), parts along dimension 0, may hold values from 1 to 8192
- seg_lengths: int32 [4, 4], P(('groups', 'replica')), parts along dimension 0, may hold values from 1 to 64, 128 in all within a row
Outputs:
- residual_out: bfloat16 [4, 64, 128, 128], P(('groups', 'replica'), 'tensor'), parts along dimension 0
- query_out: bfloat16 [4, 8192, 128], P(('groups', 'replica'), 'tensor'), parts along dimension 0
The draws below stay inside these ranges and needn't reach their ends.
There are 2 independent parts, one for each index of `groups`. The reference program is written for one: setup_inputs(seed, part) draws one part's arguments, and reference() takes and returns one part's arrays. A program takes and returns all parts, laid end to end along the dimension named above; an argument that names none is the same for every part. Nothing has to cross between parts.
Inputs may be any that keep to these rules, and one draw needn't show every extreme that they name: `seg_lengths`: each row holds the lengths of 4 segments that together fill the 128 tokens; the longest is exactly 64.
All inputs are finite; a program needn't handle non-finite values.
Results may differ from the reference program's by a relative error of at most 0.012.
Values may be sent and summed in bfloat16 or wider, within the bound.
No kernel may reach another device: no remote copies, remote signals or barrier semaphores. Data moves between devices by JAX's collectives and lax.ppermute only.
A program may use at most 256 MiB of HBM per device.

```python
import math
import jax
import jax.numpy as jnp
import numpy as np
from jax import lax

D = 8192
FF = 28672
QW = 8192
HEAD = 128
HB = 128
SEGS = 4
PREFIX = 8192
SPAN = 128
BATCH = 2
BLOCKS = 64
TSPLIT = 1
PIECE = 128
N_TENSOR = 8


def raised(result, stream_key, source, target, blocks, factor):
    owner, partner = [(jnp.arange(result.shape[dim]) // (result.shape[dim] // blocks)).reshape([-1 if axis == dim else 1 for axis in range(result.ndim)]) for dim in (source, target)]
    chosen = jax.random.permutation(stream_key, blocks)[partner]
    strong = (owner == chosen) | (owner == (partner + blocks // 2) % blocks)
    return jnp.where(strong, factor * result, result)


def shard_levels(rng, extent, pieces, smallest, top_value):
    loudness, own = 1.0, jax.random.fold_in(rng, 6)
    for position, blocks in pieces:
        steps = jnp.exp(jax.random.uniform(jax.random.fold_in(own, position), (blocks,), jnp.float32, smallest / len(pieces), top_value / len(pieces)))
        loudness = loudness * jnp.repeat(steps, extent[position] // blocks).reshape([-1 if axis == position else 1 for axis in range(len(extent))])
    return loudness


def split_up(number_of, total, limit, skew):
    loads = [(1 << 20) // math.isqrt(standing ** skew) + 1 for standing in range(2, number_of + 1)]
    spare, given = total - limit - (number_of - 1), [1] * (number_of - 1)
    while spare > 0:
        movable = [i for i in range(number_of - 1) if given[i] < limit]
        pool, left = sum([loads[i] for i in movable]), spare
        for i in movable:
            addition = min(limit - given[i], max(1, left * loads[i] // pool), spare)
            given[i] = given[i] + addition
            spare = spare - addition
    return np.array([limit] + given)


def ragged_sizes(own_key, number_of, total, reach, slope):
    if number_of == 2:
        one = jax.random.randint(own_key, (), max(1, total - reach), min(reach, total - 1) + 1)
        return jnp.stack([one, total - one])
    sizes = jnp.asarray(split_up(number_of, total, reach, slope), jnp.int32)
    pairs = (number_of - 1) // 2
    giver, receiver = sizes[1:1 + 2 * pairs:2], sizes[2:2 + 2 * pairs:2]
    slack = jnp.minimum(giver - 1, reach - receiver)
    moved = jax.random.randint(jax.random.fold_in(own_key, 1), (pairs,), 0, 1 << 20) % (slack + 1)
    sizes = sizes.at[1:1 + 2 * pairs:2].set(giver - moved).at[2:2 + 2 * pairs:2].set(receiver + moved)
    return sizes[jax.random.permutation(jax.random.fold_in(own_key, 2), number_of)]


def gaussian(own_key, extent, spread, bound, cuts=(), kind=jnp.bfloat16):
    array = jax.random.normal(own_key, extent, jnp.float32) * spread
    if len(cuts) > 0:
        array = shard_levels(own_key, extent, cuts, -0.22, 0.18) * array
    return jnp.clip(array, min=-bound, max=bound).astype(kind)


def bell_draw_with(key, dims, width, reach, cuts, heavy, kind=jnp.bfloat16):
    result = width * jax.random.normal(key, dims, jnp.float32)
    if cuts:
        result = result * shard_levels(key, dims, cuts, -0.22, 0.18)
    return jnp.clip(raised(result, jax.random.fold_in(key, 3), *heavy), -reach, reach).astype(kind)


def setup_inputs(seed: int = 0, part: int = 0) -> dict:
    arg_keys = jax.random.split(jax.random.key(seed), 8)
    own_keys = jax.random.split(jax.random.fold_in(arg_keys[7], part), 8)
    hidden = bell_draw_with(own_keys[0], (BATCH, FF, SPAN), 1.0, 6.0, ((0, 2), (1, 8)), (1, 2, 8, 2.0))
    down_weight = gaussian(arg_keys[1], (FF, D), FF ** -0.5, 0.03125, ((0, 8),))
    residual = gaussian(own_keys[2], (BATCH, TSPLIT * BLOCKS, PIECE, HB), 0.5, 3.0, ((0, 2), (1, 8)))
    norm_gain = jnp.clip(1.0 + 0.15 * jax.random.normal(arg_keys[3], (D,), jnp.float32), 0.25, 1.75)
    query_weight = gaussian(arg_keys[4], (QW, D), D ** -0.5, 0.0625, ((0, 8),))
    prefix_len = jax.random.randint(own_keys[5], (BATCH,), 1, PREFIX + 1).astype(jnp.int32)
    seg_lengths = jax.vmap(lambda own: ragged_sizes(own, SEGS, SPAN, SPAN // 2, 1))(jax.random.split(own_keys[6], BATCH)).reshape((BATCH, SEGS)).astype(jnp.int32)
    return dict(hidden=hidden, down_weight=down_weight, residual=residual, norm_gain=norm_gain, query_weight=query_weight, prefix_len=prefix_len, seg_lengths=seg_lengths)


eps_norm = 1e-05
eps_scale = 1e-06
code_top = 448.0
least_normal = 0.015625
rope_base = 500000.0

def hadamard_table(order_size):
    row_ids = lax.broadcasted_iota(jnp.int32, (order_size, order_size), 0)
    col_ids = lax.broadcasted_iota(jnp.int32, (order_size, order_size), 1)
    common = jnp.bitwise_and(row_ids, col_ids)
    parity = jnp.zeros((order_size, order_size), jnp.int32)
    for shift_bits in range(order_size.bit_length()):
        parity = parity + jnp.bitwise_and(jnp.right_shift(common, shift_bits), 1)
    sign_table = (1 - 2 * (parity % 2)).astype(jnp.float32)
    return sign_table / math.sqrt(order_size)

def grid_code(scaled):
    magnitude = jnp.maximum(jnp.abs(scaled), least_normal)
    binade = jnp.floor(jnp.log2(magnitude))
    spacing = jnp.exp2(binade - 3.0)
    return spacing * jnp.floor(scaled / spacing + 0.5)

def positions_of(prefix_one, length_row, token_count):
    seg_total = length_row.shape[0]
    before = lax.broadcasted_iota(jnp.int32, (seg_total, seg_total), 0) < lax.broadcasted_iota(jnp.int32, (seg_total, seg_total), 1)
    seg_starts = lax.optimization_barrier(jnp.sum(jnp.where(before, length_row[:, None], 0), axis=0)).astype(jnp.int32)
    token_place = lax.broadcasted_iota(jnp.int32, (token_count, seg_total), 0)
    started = token_place >= seg_starts[None, :]
    seg_start = lax.optimization_barrier(jnp.max(jnp.where(started, seg_starts[None, :], 0), axis=1)).astype(jnp.int32)
    return (prefix_one + token_place[:, 0] - seg_start).astype(jnp.float32)

def rotate_rows(projected, columns, positions):
    token_count = projected.shape[1]
    even_columns = columns.reshape(-1, 2)[:, 0]
    pair_index = even_columns % HEAD // 2
    inv_freq = jnp.exp(pair_index.astype(jnp.float32) * (-2.0 * math.log(rope_base) / HEAD))
    angles = inv_freq[:, None] * positions[None, :]
    cosine = jnp.cos(angles)
    sine_part = jnp.sin(angles)
    paired = projected.reshape(-1, 2, token_count)
    even_part = paired[:, 0]
    odd_part = paired[:, 1]
    rotated_pairs = jnp.stack([even_part * cosine - odd_part * sine_part, even_part * sine_part + odd_part * cosine], axis=1)
    return rotated_pairs.reshape(projected.shape)

def reference(hidden, down_weight, residual, norm_gain, query_weight, prefix_len, seg_lengths):
    hadamard = hadamard_table(HB)
    unit_share = FF // N_TENSOR
    blocks = D // HB
    splits = residual.shape[1] // blocks
    piece_len = residual.shape[2]
    residual_list = []
    query_list = []
    for batch_index in range(BATCH):
        hidden_one = hidden[batch_index]

        def add_block(running, block_index):
            first_row = (block_index * unit_share).astype(jnp.int32)
            rows_piece = lax.dynamic_slice_in_dim(hidden_one, first_row, unit_share, 0)
            weight_rows = lax.dynamic_slice_in_dim(down_weight, first_row, unit_share, 0)
            partial_value = lax.dot_general(rows_piece, weight_rows, (((0,), (0,)), ((), ())), preferred_element_type=jnp.float32)
            rotated = jnp.dot(partial_value.reshape(SPAN * blocks, HB), hadamard, precision=lax.Precision.HIGHEST)
            block_scale = (lax.optimization_barrier(jnp.max(jnp.abs(rotated), axis=1, keepdims=True)) + eps_scale) / code_top
            block_code = lax.optimization_barrier(grid_code(rotated / block_scale).astype(jnp.bfloat16))
            return (running + block_code.astype(jnp.float32) * block_scale, None)
        summed, _ = lax.scan(add_block, jnp.zeros((SPAN * blocks, HB), jnp.float32), jnp.arange(N_TENSOR, dtype=jnp.int32))
        restored = jnp.dot(summed, hadamard, precision=lax.Precision.HIGHEST).reshape(SPAN, D)
        stream = residual[batch_index].reshape(splits, blocks, piece_len, HB).transpose(0, 2, 1, 3).reshape(SPAN, D)
        updated = (stream.astype(jnp.float32) + restored).astype(jnp.bfloat16)
        widened = lax.optimization_barrier(updated).astype(jnp.float32)
        normed = (widened * lax.rsqrt(lax.optimization_barrier(jnp.mean(widened * widened, axis=1, keepdims=True)) + eps_norm) * norm_gain[None, :]).astype(jnp.bfloat16)
        projected = lax.dot_general(query_weight, normed, (((1,), (1,)), ((), ())), preferred_element_type=jnp.float32)
        positions = positions_of(prefix_len[batch_index], seg_lengths[batch_index], SPAN)
        columns = jnp.arange(QW, dtype=jnp.int32)
        query_one = rotate_rows(projected, columns, positions).astype(jnp.bfloat16)
        laid_out = updated.reshape(splits, piece_len, blocks, HB).transpose(0, 2, 1, 3).reshape(splits * blocks, piece_len, HB)
        residual_list.append(laid_out)
        query_list.append(query_one)
    return (jnp.stack(residual_list), jnp.stack(query_list))
```

```python
import functools
import math

import jax
import jax.numpy as jnp
import numpy as np
from jax import lax
from jax.experimental import pallas as pl
from jax.experimental.pallas import tpu as pltpu
from jax.sharding import PartitionSpec as P

HEAD = 128
HB = 128


eps_norm = 1e-05
eps_scale = 1e-06
code_top = 448.0
least_normal = 0.015625
rope_base = 500000.0

bf16 = jnp.bfloat16
f32 = jnp.float32


def hadamard_table(order_size):
    row_ids = lax.broadcasted_iota(jnp.int32, (order_size, order_size), 0)
    col_ids = lax.broadcasted_iota(jnp.int32, (order_size, order_size), 1)
    common = jnp.bitwise_and(row_ids, col_ids)
    parity = jnp.zeros((order_size, order_size), jnp.int32)
    for shift_bits in range(order_size.bit_length()):
        parity = parity + jnp.bitwise_and(jnp.right_shift(common, shift_bits), 1)
    sign_table = (1 - 2 * (parity % 2)).astype(jnp.float32)
    return sign_table / math.sqrt(order_size)


def hadamard_signs():
    ids = np.arange(HB)
    common = ids[:, None] & ids[None, :]
    parity = np.zeros_like(common)
    for shift_bits in range(HB.bit_length()):
        parity += (common >> shift_bits) & 1
    signs = (1 - 2 * (parity % 2)).astype(np.float32)
    return jnp.asarray(np.concatenate([signs, signs], axis=0)).astype(bf16)


def grid_code(scaled):
    magnitude = jnp.maximum(jnp.abs(scaled), least_normal)
    binade = jnp.floor(jnp.log2(magnitude))
    spacing = jnp.exp2(binade - 3.0)
    return spacing * jnp.floor(scaled / spacing + 0.5)


def positions_of(prefix_one, length_row, token_count):
    seg_total = length_row.shape[0]
    before = lax.broadcasted_iota(jnp.int32, (seg_total, seg_total), 0) < lax.broadcasted_iota(
        jnp.int32, (seg_total, seg_total), 1
    )
    seg_starts = jnp.sum(jnp.where(before, length_row[:, None], 0), axis=0)
    token_place = lax.broadcasted_iota(jnp.int32, (token_count, seg_total), 0)
    started = token_place >= seg_starts[None, :]
    seg_start = jnp.max(jnp.where(started, seg_starts[None, :], 0), axis=1)
    return (prefix_one + token_place[:, 0] - seg_start).astype(jnp.float32)


def rotate_rows(projected, columns, positions):
    token_count = projected.shape[1]
    even_columns = columns.reshape(-1, 2)[:, 0]
    pair_index = even_columns % HEAD // 2
    inv_freq = jnp.exp(pair_index.astype(jnp.float32) * (-2.0 * math.log(rope_base) / HEAD))
    angles = inv_freq[:, None] * positions[None, :]
    cosine = jnp.cos(angles)
    sine_part = jnp.sin(angles)
    paired = projected.reshape(-1, 2, token_count)
    even_part = paired[:, 0]
    odd_part = paired[:, 1]
    rotated_pairs = jnp.stack(
        [even_part * cosine - odd_part * sine_part, even_part * sine_part + odd_part * cosine],
        axis=1,
    )
    return rotated_pairs.reshape(projected.shape)


def local_general(hidden, down_weight, residual, norm_gain, query_weight, prefix_len, seg_lengths):
    members = lax.axis_size("tensor")
    span_len = hidden.shape[2]
    model_width = down_weight.shape[1]
    blocks = model_width // HB
    splits = max(1, members // blocks)
    piece_len = span_len // splits
    item_total = splits * blocks
    per_device = item_total // members
    hadamard = hadamard_table(HB)
    partial_value = lax.dot_general(
        hidden[0], down_weight, (((0,), (0,)), ((), ())), preferred_element_type=jnp.float32
    )
    partial_value = partial_value.reshape(splits, piece_len, blocks, HB).transpose(0, 2, 1, 3)
    rotated = jnp.einsum("sbch,hk->sbck", partial_value, hadamard, precision=lax.Precision.HIGHEST)
    block_scale = (jnp.max(jnp.abs(rotated), axis=3, keepdims=True) + eps_scale) / code_top
    block_code = grid_code(rotated / block_scale).astype(jnp.bfloat16)
    sent_codes = block_code.reshape(members, per_device, piece_len, HB)
    sent_scales = block_scale.reshape(members, per_device, piece_len)
    got_codes = lax.all_to_all(sent_codes, "tensor", split_axis=0, concat_axis=0, tiled=True)
    got_scales = lax.all_to_all(
        sent_scales.astype(jnp.bfloat16), "tensor", split_axis=0, concat_axis=0, tiled=True
    ).astype(sent_scales.dtype)
    running = jnp.sum(got_codes.astype(jnp.float32) * got_scales[..., None], axis=0)
    item_count = running.shape[0]
    unrotated = jnp.dot(running.reshape(-1, HB), hadamard, precision=lax.Precision.HIGHEST)
    restored = unrotated.reshape(item_count, piece_len, HB)
    updated = (residual[0].astype(jnp.float32) + restored).astype(jnp.bfloat16)
    gathered = lax.all_gather(updated, "tensor", axis=0, tiled=True)
    widened = gathered.astype(jnp.float32).reshape(splits, blocks, piece_len, HB)
    mean_square = jnp.mean(widened * widened, axis=(1, 3), keepdims=True)
    gain_blocks = norm_gain.reshape(1, blocks, 1, HB)
    normed = (widened * lax.rsqrt(mean_square + eps_norm) * gain_blocks).astype(jnp.bfloat16)
    column_count = query_weight.shape[0]
    weight_blocks = query_weight.reshape(column_count, blocks, HB)
    projected = jnp.einsum(
        "qbh,sbch->qsc", weight_blocks, normed, preferred_element_type=jnp.float32
    ).reshape(column_count, span_len)
    positions = positions_of(prefix_len[0], seg_lengths[0], span_len)
    columns = lax.axis_index("tensor") * column_count + lax.iota(jnp.int32, column_count)
    query_one = rotate_rows(projected, columns, positions).astype(jnp.bfloat16)
    return (updated[None], query_one[None])


def split_dot(value, signs):
    high = value.astype(bf16)
    low = (value - high.astype(f32)).astype(bf16)
    return jnp.dot(jnp.concatenate([high, low], axis=1), signs, preferred_element_type=f32)


def down_kernel(counts, units, rows_ref, weight_ref, signs_ref, *outs):
    step = pl.program_id(0)
    tiles = counts["tiles"]
    per_tile = counts["per_tile"]
    total = jnp.dot(rows_ref[...], weight_ref[...], preferred_element_type=f32)
    signs = signs_ref[...]
    values = []
    for j in range(per_tile):
        rotated = split_dot(total[:, j * HB : (j + 1) * HB], signs)
        top = jnp.max(jnp.abs(rotated), axis=1, keepdims=True) * (1.0 / math.sqrt(HB)) + eps_scale
        scaled = rotated * ((code_top / math.sqrt(HB)) / top)
        magnitude = jnp.maximum(jnp.abs(scaled), least_normal)
        binade = jnp.floor(jnp.log2(magnitude))
        code = jnp.exp2(binade - 3.0) * jnp.floor(scaled * jnp.exp2(3.0 - binade) + 0.5)
        values.append(code * (top * (1.0 / code_top)))
    for k, out in enumerate(outs):

        def store(out=out):
            for j in range(per_tile):
                out[j] = values[j].astype(out.dtype)

        if len(outs) == 1:
            store()
        else:
            pl.when(step // tiles == k)(store)


def down_units(rows, down_weight, signs, units, dtypes):
    count = len(dtypes)
    tokens, depth = rows.shape
    unit_width = down_weight.shape[1] // 8
    tile = 256
    tiles = unit_width // tile
    per_tile = tile // HB
    unit_blocks = unit_width // HB
    out_specs = [
        pl.BlockSpec(
            (per_tile, tokens, HB),
            functools.partial(lambda i, s, k: (jnp.clip(i - k * tiles, 0, tiles - 1), 0, 0), k=k),
        )
        for k in range(count)
    ]
    return pl.pallas_call(
        functools.partial(down_kernel, dict(tiles=tiles, per_tile=per_tile)),
        grid_spec=pltpu.PrefetchScalarGridSpec(
            num_scalar_prefetch=1,
            grid=(count * tiles,),
            in_specs=[
                pl.BlockSpec((tokens, depth), lambda i, s: (0, 0)),
                pl.BlockSpec((depth, tile), lambda i, s: (0, s[i // tiles] * tiles + i % tiles)),
                pl.BlockSpec((2 * HB, HB), lambda i, s: (0, 0)),
            ],
            out_specs=out_specs,
        ),
        out_shape=[jax.ShapeDtypeStruct((unit_blocks, tokens, HB), d) for d in dtypes],
        compiler_params=pltpu.CompilerParams(vmem_limit_bytes=24 << 20),
        cost_estimate=pl.CostEstimate(
            flops=2 * tokens * depth * unit_width * count,
            bytes_accessed=2 * depth * unit_width * count,
            transcendentals=0,
        ),
        name="down_units",
    )(jnp.stack(units), rows, down_weight, signs)


def update_kernel(own_ref, a_ref, b_ref, c_ref, residual_ref, signs_ref, out_ref):
    signs = signs_ref[...]
    for j in range(own_ref.shape[0]):
        summed = own_ref[j] + a_ref[j].astype(f32) + b_ref[j].astype(f32) + c_ref[j].astype(f32)
        restored = split_dot(summed, signs) * (1.0 / math.sqrt(HB))
        out_ref[j] = (residual_ref[j].astype(f32) + restored).astype(out_ref.dtype)


def update(own, a, b, c, residual, signs):
    return pl.pallas_call(
        update_kernel,
        out_shape=jax.ShapeDtypeStruct(residual.shape, residual.dtype),
        compiler_params=pltpu.CompilerParams(vmem_limit_bytes=24 << 20),
        name="update",
    )(own, a, b, c, residual, signs)


def query_kernel(info, units, *refs):
    count, tiles, tile, first, last = (info[n] for n in ("count", "tiles", "tile", "first", "last"))
    refs = list(refs)
    stream = [refs.pop(0) for _ in range(count)]
    gains = [refs.pop(0) for _ in range(count)]
    weight_ref = refs.pop(0)
    if not first:
        acc_in, square_in = refs.pop(0), refs.pop(0)
    if last:
        cos_ref, sin_ref, out_ref, acc_ref, square_ref, factor = refs
    else:
        acc_ref, square_ref, factor = refs
    step = pl.program_id(0)
    blocks = stream[0].shape[0]
    for k in range(count):

        @pl.when(step == k * tiles)
        def _(k=k):
            squares = None
            for j in range(blocks):
                value = stream[k][j].astype(f32)
                squares = value * value if squares is None else squares + value * value
                factor[:, j * HB : (j + 1) * HB] = (value * gains[k][j : j + 1, :]).astype(bf16)
            if k > 0:
                square_ref[...] += squares
            elif first:
                square_ref[...] = squares
            else:
                square_ref[...] = square_in[...] + squares

    product = lax.dot_general(
        weight_ref[...], factor[...], (((1,), (1,)), ((), ())), preferred_element_type=f32
    )
    here = pl.ds(pl.multiple_of((step % tiles) * tile, tile), tile)

    @pl.when(step < tiles)
    def _():
        if first:
            acc_ref[here, :] = product
        else:
            acc_ref[here, :] = acc_in[here, :] + product

    if count > 1:

        @pl.when(step >= tiles)
        def _():
            acc_ref[here, :] += product

    if last:

        @pl.when(step >= (count - 1) * tiles)
        def _():
            mean_square = jnp.sum(square_ref[...].T, axis=0, keepdims=True) * (1.0 / info["width"])
            root = lax.rsqrt(mean_square + eps_norm)
            even = lax.broadcasted_iota(jnp.int32, (HEAD, HB), 0) % 2 == 0
            for h in range(tile // HEAD):
                rows = pl.ds(pl.multiple_of((step % tiles) * tile + h * HEAD, HEAD), HEAD)
                value = acc_ref[rows, :] * root
                up, down = pltpu.roll(value, HEAD - 1, 0), pltpu.roll(value, 1, 0)
                other = jnp.where(even, up, down)
                out_ref[h * HEAD : (h + 1) * HEAD, :] = (value * cos_ref[...] + other * sin_ref[...]).astype(out_ref.dtype)


def query_units(streams, units, gain, query_weight, carried=None, tables=None):
    count = len(streams)
    blocks, tokens, _ = streams[0].shape
    columns, width = query_weight.shape
    unit_width = blocks * HB
    tile = 256
    tiles = columns // tile
    first, last = carried is None, tables is not None
    info = dict(count=count, tiles=tiles, tile=tile, first=first, last=last, width=width)
    whole = lambda shape: pl.BlockSpec(shape, lambda i, s: (0,) * len(shape))
    in_specs = [whole((blocks, tokens, HB))] * count
    in_specs += [pl.BlockSpec((blocks, HB), functools.partial(lambda i, s, k: (s[k], 0), k=k)) for k in range(count)]
    in_specs += [pl.BlockSpec((tile, unit_width), lambda i, s: (i % tiles, s[i // tiles]))]
    args = [*streams, *([gain] * count), query_weight]
    if not first:
        in_specs += [whole((columns, tokens)), whole((tokens, HB))]
        args += list(carried)
    scratch = [pltpu.VMEM((tokens, unit_width), bf16)]
    state = [((columns, tokens), f32), ((tokens, HB), f32)]
    if last:
        in_specs += [whole((HEAD, tokens))] * 2
        args += list(tables)
        out_specs = pl.BlockSpec((tile, tokens), lambda i, s: (jnp.maximum(i - (count - 1) * tiles, 0), 0))
        out_shape = jax.ShapeDtypeStruct((columns, tokens), bf16)
        scratch = [pltpu.VMEM(s, d) for s, d in state] + scratch
    else:
        out_specs = [whole(s) for s, _ in state]
        out_shape = [jax.ShapeDtypeStruct(s, d) for s, d in state]
    return pl.pallas_call(
        functools.partial(query_kernel, info),
        grid_spec=pltpu.PrefetchScalarGridSpec(
            num_scalar_prefetch=1,
            grid=(count * tiles,),
            in_specs=in_specs,
            out_specs=out_specs,
            scratch_shapes=scratch,
        ),
        out_shape=out_shape,
        compiler_params=pltpu.CompilerParams(vmem_limit_bytes=24 << 20),
        cost_estimate=pl.CostEstimate(
            flops=2 * tokens * columns * unit_width * count,
            bytes_accessed=2 * columns * unit_width * count,
            transcendentals=0,
        ),
        name="query_units",
    )(jnp.stack(units), *args)


def rotary_tables(positions):
    row_ids = jnp.arange(HEAD, dtype=jnp.int32)
    inv_freq = jnp.exp((row_ids // 2).astype(f32) * (-2.0 * math.log(rope_base) / HEAD))
    angles = inv_freq[:, None] * positions[None, :]
    sign = jnp.where(row_ids % 2 == 0, -1.0, 1.0).astype(f32)
    return jnp.cos(angles), jnp.sin(angles) * sign[:, None]


def line_pairs(pairs):
    return [(2 * a + x, 2 * b + x) for a, b in pairs for x in range(2)]


ACROSS = [(t, t ^ 1) for t in range(8)]
TWINS = line_pairs([(0, 1), (1, 0), (2, 3), (3, 2)])
MIDDLE = line_pairs([(1, 2), (2, 1)])
INWARD = line_pairs([(0, 1), (3, 2)])
OUTWARD = line_pairs([(1, 0), (2, 3)])


def send(value, pairs):
    return lax.ppermute(value.astype(bf16), "tensor", pairs)


def local_eight(hidden, down_weight, residual, norm_gain, query_weight, prefix_len, seg_lengths):
    place = lax.axis_index("tensor").astype(jnp.int32)
    z, x = place // 2, place % 2
    tokens = hidden.shape[2]
    slot = [z, z ^ 1, jnp.where(z < 2, 2, 1), jnp.where(z < 2, 3, 0)]
    mine = [2 * s + x for s in slot]
    theirs = [2 * s + 1 - x for s in slot]
    signs = hadamard_signs()
    rows = hidden[0].T

    def down(units, dtypes):
        return down_units(rows, down_weight, signs, units, dtypes)

    out3, = down([theirs[3]], [bf16])
    got3 = send(out3, ACROSS)
    own3, out2 = down([mine[3], theirs[2]], [f32, bf16])
    got2 = send(out2, ACROSS)
    own2, out1 = down([mine[2], theirs[1]], [f32, bf16])
    got1 = send(out1, ACROSS)
    own1, out0 = down([mine[1], theirs[0]], [f32, bf16])
    got0 = send(out0, ACROSS)
    own0, = down([mine[0]], [f32])

    sum3 = own3 + got3.astype(f32)
    sum3 = sum3 + send(sum3, INWARD).astype(f32)
    sum2 = own2 + got2.astype(f32)
    sum2 = sum2 + send(sum2, INWARD).astype(f32)
    sum1 = own1 + got1.astype(f32) + send(sum3, MIDDLE).astype(f32)
    from2 = send(sum2, MIDDLE)
    from1 = send(sum1, TWINS)
    updated = update(own0, got0, from2, from1, residual[0], signs)

    gain = norm_gain.reshape(-1, HB)
    tables = rotary_tables(positions_of(prefix_len[0], seg_lengths[0], tokens))
    unit0 = updated
    unit1 = send(unit0, TWINS)
    inner2 = send(unit0, MIDDLE)
    inner3 = send(unit1, MIDDLE)
    unit2 = inner2 + send(inner2, OUTWARD)
    unit3 = inner3 + send(inner3, OUTWARD)
    side0 = send(unit0, ACROSS)
    side1 = send(unit1, ACROSS)
    side2 = send(unit2, ACROSS)
    side3 = send(unit3, ACROSS)
    state = query_units([unit0], [mine[0]], gain, query_weight)
    state = query_units([side0, unit1], [theirs[0], mine[1]], gain, query_weight, state)
    state = query_units([side1, unit2], [theirs[1], mine[2]], gain, query_weight, state)
    state = query_units([side2, unit3], [theirs[2], mine[3]], gain, query_weight, state)
    query_one = query_units([side3], [theirs[3]], gain, query_weight, state, tables)
    return (updated[None], query_one[None])


def solution(mesh):
    in_specs = (
        P(("groups", "replica"), "tensor", None),
        P("tensor", None),
        P(("groups", "replica"), "tensor", None, None),
        P(),
        P("tensor", None),
        P(("groups", "replica")),
        P(("groups", "replica"), None),
    )
    out_specs = (
        P(("groups", "replica"), "tensor", None, None),
        P(("groups", "replica"), "tensor", None),
    )
    local = local_eight if mesh.shape["tensor"] == 8 else local_general
    return jax.shard_map(local, mesh=mesh, in_specs=in_specs, out_specs=out_specs, check_vma=False)
```

```python
import functools
import math

import jax
import jax.numpy as jnp
from jax import lax
from jax.experimental import pallas as pl
from jax.experimental.pallas import tpu as pltpu
from jax.sharding import PartitionSpec as P

HEAD = 128
HB = 128


eps_norm = 1e-05
eps_scale = 1e-06
code_top = 448.0
least_normal = 0.015625
rope_base = 500000.0

bf16 = jnp.bfloat16
f32 = jnp.float32


def hadamard_table(order_size):
    row_ids = lax.broadcasted_iota(jnp.int32, (order_size, order_size), 0)
    col_ids = lax.broadcasted_iota(jnp.int32, (order_size, order_size), 1)
    common = jnp.bitwise_and(row_ids, col_ids)
    parity = jnp.zeros((order_size, order_size), jnp.int32)
    for shift_bits in range(order_size.bit_length()):
        parity = parity + jnp.bitwise_and(jnp.right_shift(common, shift_bits), 1)
    sign_table = (1 - 2 * (parity % 2)).astype(jnp.float32)
    return sign_table / math.sqrt(order_size)


def hadamard_signs():
    row_ids = lax.broadcasted_iota(jnp.int32, (2 * HB, HB), 0)
    col_ids = lax.broadcasted_iota(jnp.int32, (2 * HB, HB), 1)
    common = jnp.bitwise_and(row_ids, col_ids)
    for shift_bits in (4, 2, 1):
        common = jnp.bitwise_xor(common, jnp.right_shift(common, shift_bits))
    return (1 - 2 * jnp.bitwise_and(common, 1)).astype(f32).astype(bf16)


def grid_code(scaled):
    magnitude = jnp.maximum(jnp.abs(scaled), least_normal)
    binade = jnp.floor(jnp.log2(magnitude))
    spacing = jnp.exp2(binade - 3.0)
    return spacing * jnp.floor(scaled / spacing + 0.5)


def positions_of(prefix_one, length_row, token_count):
    seg_total = length_row.shape[0]
    before = lax.broadcasted_iota(jnp.int32, (seg_total, seg_total), 0) < lax.broadcasted_iota(
        jnp.int32, (seg_total, seg_total), 1
    )
    seg_starts = jnp.sum(jnp.where(before, length_row[:, None], 0), axis=0)
    token_place = lax.broadcasted_iota(jnp.int32, (token_count, seg_total), 0)
    started = token_place >= seg_starts[None, :]
    seg_start = jnp.max(jnp.where(started, seg_starts[None, :], 0), axis=1)
    return (prefix_one + token_place[:, 0] - seg_start).astype(jnp.float32)


def rotate_rows(projected, columns, positions):
    token_count = projected.shape[1]
    even_columns = columns.reshape(-1, 2)[:, 0]
    pair_index = even_columns % HEAD // 2
    inv_freq = jnp.exp(pair_index.astype(jnp.float32) * (-2.0 * math.log(rope_base) / HEAD))
    angles = inv_freq[:, None] * positions[None, :]
    cosine = jnp.cos(angles)
    sine_part = jnp.sin(angles)
    paired = projected.reshape(-1, 2, token_count)
    even_part = paired[:, 0]
    odd_part = paired[:, 1]
    rotated_pairs = jnp.stack(
        [even_part * cosine - odd_part * sine_part, even_part * sine_part + odd_part * cosine],
        axis=1,
    )
    return rotated_pairs.reshape(projected.shape)


def local_general(hidden, down_weight, residual, norm_gain, query_weight, prefix_len, seg_lengths):
    members = lax.axis_size("tensor")
    span_len = hidden.shape[2]
    model_width = down_weight.shape[1]
    blocks = model_width // HB
    splits = max(1, members // blocks)
    piece_len = span_len // splits
    item_total = splits * blocks
    per_device = item_total // members
    hadamard = hadamard_table(HB)
    partial_value = lax.dot_general(
        hidden[0], down_weight, (((0,), (0,)), ((), ())), preferred_element_type=jnp.float32
    )
    partial_value = partial_value.reshape(splits, piece_len, blocks, HB).transpose(0, 2, 1, 3)
    rotated = jnp.einsum("sbch,hk->sbck", partial_value, hadamard, precision=lax.Precision.HIGHEST)
    block_scale = (jnp.max(jnp.abs(rotated), axis=3, keepdims=True) + eps_scale) / code_top
    block_code = grid_code(rotated / block_scale).astype(jnp.bfloat16)
    sent_codes = block_code.reshape(members, per_device, piece_len, HB)
    sent_scales = block_scale.reshape(members, per_device, piece_len)
    got_codes = lax.all_to_all(sent_codes, "tensor", split_axis=0, concat_axis=0, tiled=True)
    got_scales = lax.all_to_all(
        sent_scales.astype(jnp.bfloat16), "tensor", split_axis=0, concat_axis=0, tiled=True
    ).astype(sent_scales.dtype)
    running = jnp.sum(got_codes.astype(jnp.float32) * got_scales[..., None], axis=0)
    item_count = running.shape[0]
    unrotated = jnp.dot(running.reshape(-1, HB), hadamard, precision=lax.Precision.HIGHEST)
    restored = unrotated.reshape(item_count, piece_len, HB)
    updated = (residual[0].astype(jnp.float32) + restored).astype(jnp.bfloat16)
    gathered = lax.all_gather(updated, "tensor", axis=0, tiled=True)
    widened = gathered.astype(jnp.float32).reshape(splits, blocks, piece_len, HB)
    mean_square = jnp.mean(widened * widened, axis=(1, 3), keepdims=True)
    gain_blocks = norm_gain.reshape(1, blocks, 1, HB)
    normed = (widened * lax.rsqrt(mean_square + eps_norm) * gain_blocks).astype(jnp.bfloat16)
    column_count = query_weight.shape[0]
    weight_blocks = query_weight.reshape(column_count, blocks, HB)
    projected = jnp.einsum(
        "qbh,sbch->qsc", weight_blocks, normed, preferred_element_type=jnp.float32
    ).reshape(column_count, span_len)
    positions = positions_of(prefix_len[0], seg_lengths[0], span_len)
    columns = lax.axis_index("tensor") * column_count + lax.iota(jnp.int32, column_count)
    query_one = rotate_rows(projected, columns, positions).astype(jnp.bfloat16)
    return (updated[None], query_one[None])


def split_dot(value, signs):
    high = value.astype(bf16)
    low = (value - high.astype(f32)).astype(bf16)
    return jnp.dot(jnp.concatenate([high, low], axis=1), signs, preferred_element_type=f32)


def coded(total, signs):
    for j in range(total.shape[1] // HB):
        rotated = split_dot(total[:, j * HB : (j + 1) * HB], signs)
        top = jnp.max(jnp.abs(rotated), axis=1, keepdims=True) * (1.0 / math.sqrt(HB)) + eps_scale
        scaled = rotated * ((code_top / math.sqrt(HB)) / top)
        anchor = jnp.maximum(jnp.abs(scaled), least_normal) * (2.0**20 - 4.0)
        code = (scaled + anchor) - anchor
        yield code * (top * (1.0 / code_top))


def down_kernel(count, first, chunk, units, *refs):
    if first:
        rows_ref, weight_ref, out, turned, signs_out, held, sems, held_rows, row_sem = refs
        outs = [out]
    else:
        rows_ref, weight_ref, signs_ref, *outs, held, sems = refs
    depth, width = held.shape[1:]
    chunks = depth // chunk

    def fetch(k, c):
        here = pl.ds(c * chunk, chunk)
        columns = pl.ds(pl.multiple_of(units[k] * width, width), width)
        return pltpu.make_async_copy(weight_ref.at[here, columns], held.at[k, here], sems.at[k, c])

    if first:
        bring = pltpu.make_async_copy(rows_ref, held_rows, row_sem)
        bring.start()
    for k in range(count):
        for c in range(chunks):
            fetch(k, c).start()
    if first:
        signs = hadamard_signs()
        signs_out[...] = signs
        bring.wait()
    else:
        signs = signs_ref[...]
    for k in range(count):
        total = None
        for c in range(chunks):
            here = slice(c * chunk, (c + 1) * chunk)
            if first:
                rows = held_rows[here, :].T
                turned[:, here] = rows
            else:
                rows = rows_ref[:, here]
            fetch(k, c).wait()
            product = jnp.dot(rows, held[k, here, :], preferred_element_type=f32)
            total = product if total is None else total + product
        for j, value in enumerate(coded(total, signs)):
            outs[k][j] = value.astype(outs[k].dtype)


def down_units(rows, down_weight, signs, units, dtypes):
    count = len(dtypes)
    first = signs is None
    tokens, depth = rows.shape[::-1] if first else rows.shape
    unit_width = down_weight.shape[1] // 8
    chunk = 512 if depth % 512 == 0 else depth
    vmem = pl.BlockSpec(memory_space=pltpu.VMEM)
    hbm = pl.BlockSpec(memory_space=pltpu.HBM)
    out_shape = [jax.ShapeDtypeStruct((unit_width // HB, tokens, HB), d) for d in dtypes]
    scratch = [
        pltpu.VMEM((count, depth, unit_width), bf16),
        pltpu.SemaphoreType.DMA((count, depth // chunk)),
    ]
    if first:
        out_shape.append(jax.ShapeDtypeStruct((tokens, depth), bf16))
        out_shape.append(jax.ShapeDtypeStruct((2 * HB, HB), bf16))
        scratch += [pltpu.VMEM((depth, tokens), bf16), pltpu.SemaphoreType.DMA]
        args, in_specs = (rows, down_weight), [hbm, hbm]
    else:
        args, in_specs = (rows, down_weight, signs), [vmem, hbm, vmem]
    return pl.pallas_call(
        functools.partial(down_kernel, count, first, chunk),
        in_specs=[pl.BlockSpec(memory_space=pltpu.SMEM), *in_specs],
        out_specs=[vmem] * len(out_shape),
        out_shape=out_shape,
        scratch_shapes=scratch,
        compiler_params=pltpu.CompilerParams(vmem_limit_bytes=(48 if first else 32) << 20),
        cost_estimate=pl.CostEstimate(
            flops=2 * tokens * depth * unit_width * count,
            bytes_accessed=2 * depth * unit_width * count,
            transcendentals=0,
        ),
        name="down_units",
    )(jnp.stack(units), *args)


def update_kernel(own_ref, a_ref, b_ref, c_ref, residual_ref, signs_ref, out_ref, turned_ref):
    signs = signs_ref[...]
    for j in range(own_ref.shape[0]):
        summed = own_ref[j] + a_ref[j].astype(f32) + b_ref[j].astype(f32) + c_ref[j].astype(f32)
        restored = split_dot(summed, signs) * (1.0 / math.sqrt(HB))
        value = (residual_ref[j].astype(f32) + restored).astype(out_ref.dtype)
        out_ref[j] = value
        turned_ref[j] = value.T


def update(own, a, b, c, residual, signs):
    vmem = pl.BlockSpec(memory_space=pltpu.VMEM)
    blocks, tokens, _ = residual.shape
    return pl.pallas_call(
        update_kernel,
        in_specs=[vmem] * 6,
        out_specs=[vmem, vmem],
        out_shape=[
            jax.ShapeDtypeStruct(residual.shape, residual.dtype),
            jax.ShapeDtypeStruct((blocks, HB, tokens), residual.dtype),
        ],
        compiler_params=pltpu.CompilerParams(vmem_limit_bytes=24 << 20),
        name="update",
    )(own, a, b, c, residual, signs)


def query_kernel(info, units, *refs):
    count, chunk, first, last = (info[n] for n in ("count", "chunk", "first", "last"))
    refs = list(refs)
    streams = [refs.pop(0) for _ in range(count)]
    gain_ref, weight_ref = refs.pop(0), refs.pop(0)
    if not first:
        acc_in, square_in = refs.pop(0), refs.pop(0)
    if last:
        cos_ref, sin_ref, out_ref, held, sems = refs
    else:
        acc_ref, square_ref, held, sems = refs
    blocks, _, tokens = streams[0].shape
    columns, width = held.shape[1:]
    chunks = columns // chunk

    def fetch(k, c):
        here = pl.ds(c * chunk, chunk)
        place = pl.ds(pl.multiple_of(units[k] * width, width), width)
        return pltpu.make_async_copy(weight_ref.at[here, place], held.at[k, here], sems.at[k, c])

    for c in range(chunks):
        for k in range(count):
            fetch(k, c).start()
    squares = None if first else square_in[...]
    factors = []
    for k in range(count):
        parts = []
        gains = gain_ref[pl.ds(pl.multiple_of(units[k] * blocks, blocks), blocks), :].T
        for j in range(blocks):
            value = streams[k][j].astype(f32)
            squares = value * value if squares is None else squares + value * value
            parts.append((value * gains[:, j : j + 1]).astype(bf16))
        factors.append(jnp.concatenate(parts, axis=0))
    if last:
        mean_square = jnp.sum(squares, axis=0, keepdims=True) * (1.0 / info["width"])
        root = lax.rsqrt(mean_square + eps_norm)
        even = lax.broadcasted_iota(jnp.int32, (HEAD, tokens), 0) % 2 == 0
    else:
        square_ref[...] = squares
    for c in range(chunks):
        here = slice(c * chunk, (c + 1) * chunk)
        total = None if first else acc_in[here, :]
        for k in range(count):
            fetch(k, c).wait()
            product = jnp.dot(held[k, here, :], factors[k], preferred_element_type=f32)
            total = product if total is None else total + product
        if not last:
            acc_ref[here, :] = total
            continue
        for h in range(chunk // HEAD):
            value = total[h * HEAD : (h + 1) * HEAD, :] * root
            other = jnp.where(even, pltpu.roll(value, HEAD - 1, 0), pltpu.roll(value, 1, 0))
            rotated = value * cos_ref[...] + other * sin_ref[...]
            out_ref[c * chunk + h * HEAD : c * chunk + (h + 1) * HEAD, :] = rotated.astype(out_ref.dtype)


def query_units(streams, units, gain, query_weight, carried=None, tables=None):
    count = len(streams)
    blocks, _, tokens = streams[0].shape
    columns, width = query_weight.shape
    unit_width = blocks * HB
    chunk = 256
    first, last = carried is None, tables is not None
    info = dict(count=count, chunk=chunk, first=first, last=last, width=width)
    vmem = pl.BlockSpec(memory_space=pltpu.VMEM)
    args = [jnp.stack(units), *streams, gain, query_weight, *(carried or ()), *(tables or ())]
    in_specs = [pl.BlockSpec(memory_space=pltpu.SMEM)] + [vmem] * (len(args) - 1)
    in_specs[count + 2] = pl.BlockSpec(memory_space=pltpu.HBM)
    if last:
        out_specs, out_shape = vmem, jax.ShapeDtypeStruct((columns, tokens), bf16)
    else:
        out_specs = [vmem, vmem]
        out_shape = [jax.ShapeDtypeStruct((columns, tokens), f32), jax.ShapeDtypeStruct((HB, tokens), f32)]
    return pl.pallas_call(
        functools.partial(query_kernel, info),
        in_specs=in_specs,
        out_specs=out_specs,
        out_shape=out_shape,
        scratch_shapes=[
            pltpu.VMEM((count, columns, unit_width), bf16),
            pltpu.SemaphoreType.DMA((count, columns // chunk)),
        ],
        compiler_params=pltpu.CompilerParams(vmem_limit_bytes=50 << 20),
        cost_estimate=pl.CostEstimate(
            flops=2 * tokens * columns * unit_width * count,
            bytes_accessed=2 * columns * unit_width * count,
            transcendentals=0,
        ),
        name="query_units",
    )(*args)


def rotary_tables(positions):
    row_ids = jnp.arange(HEAD, dtype=jnp.int32)
    inv_freq = jnp.exp((row_ids // 2).astype(f32) * (-2.0 * math.log(rope_base) / HEAD))
    angles = inv_freq[:, None] * positions[None, :]
    sign = jnp.where(row_ids % 2 == 0, -1.0, 1.0).astype(f32)
    return jnp.cos(angles), jnp.sin(angles) * sign[:, None]


def pairs_of(partner):
    found = []
    for z in range(4):
        for x in range(2):
            for core in range(2):
                pz, px, pcore = partner(z, x, core)
                found.append(((2 * z + x) * 2 + core, (2 * pz + px) * 2 + pcore))
    return found


ACROSS = pairs_of(lambda z, x, core: (z, 1 - x, core))
TWINS = pairs_of(lambda z, x, core: (z ^ 1, x, core))
MIDDLE = pairs_of(lambda z, x, core: (3 - z, x, core) if z in (1, 2) else (z, x, 1 - core))


def after(*values):
    return lax.optimization_barrier(values)


def send(value, pairs):
    return lax.ppermute(value.astype(bf16), ("tensor", "replica"), pairs)


def local_eight(hidden, down_weight, residual, norm_gain, query_weight, prefix_len, seg_lengths):
    place = lax.axis_index("tensor").astype(jnp.int32)
    z, x = place // 2, place % 2
    tokens = hidden.shape[2]
    slot = [z, z ^ 1, jnp.where(z < 2, 2, 1), jnp.where(z < 2, 3, 0)]
    mine = [2 * s + x for s in slot]
    theirs = [2 * s + 1 - x for s in slot]
    inner = (z == 1) | (z == 2)

    def down(units, dtypes, rows):
        return down_units(rows, down_weight, signs, units, dtypes)

    def only(here, value):
        return jnp.where(here, value, jnp.zeros_like(value))

    out3, rows, signs = down_units(hidden[0], down_weight, None, [theirs[3]], [bf16])
    got3 = send(out3, ACROSS)
    own3, out2 = down([mine[3], theirs[2]], [f32, bf16], rows)
    got2 = send(out2, ACROSS)
    part3, rows = after((own3 + got3).astype(bf16), rows)
    add3 = only(inner, send(part3, TWINS))
    own2, out1 = down([mine[2], theirs[1]], [f32, bf16], rows)
    got1 = send(out1, ACROSS)
    part2 = (own2 + got2).astype(bf16)
    add2 = only(inner, send(part2, TWINS))
    part3 = (own3 + got3 + add3).astype(bf16)
    part2, part3, rows = after(part2, part3, rows)
    add1 = only(inner, send(part3, MIDDLE))
    own1, out0 = down([mine[1], theirs[0]], [f32, bf16], rows)
    got0 = send(out0, ACROSS)
    part1 = (own1 + got1 + add1).astype(bf16)
    part2 = only(inner, (own2 + got2 + add2).astype(bf16))
    part1, part2, rows = after(part1, part2, rows)
    from1 = send(part1, TWINS)
    from2 = send(part2, MIDDLE)
    own0, = down([mine[0]], [f32], rows)
    updated, unit0 = update(own0, got0, from2, from1, residual[0], signs)

    gain = norm_gain.reshape(-1, HB)
    tables = rotary_tables(positions_of(prefix_len[0], seg_lengths[0], tokens))
    unit1 = send(unit0, TWINS)
    inner2 = send(unit0, MIDDLE)
    side0 = send(unit0, ACROSS)
    state = query_units([unit0], [mine[0]], gain, query_weight)
    unit1, state = after(unit1, state)
    inner3 = send(unit1, MIDDLE)
    unit2 = jnp.where(inner, inner2, send(inner2, TWINS))
    side1 = send(unit1, ACROSS)
    state = query_units([side0, unit1], [theirs[0], mine[1]], gain, query_weight, state)
    unit2, inner3, state = after(unit2, inner3, state)
    unit3 = jnp.where(inner, inner3, send(inner3, TWINS))
    side2 = send(unit2, ACROSS)
    state = query_units([side1, unit2], [theirs[1], mine[2]], gain, query_weight, state)
    unit3, state = after(unit3, state)
    side3 = send(unit3, ACROSS)
    state = query_units([side2, unit3], [theirs[2], mine[3]], gain, query_weight, state)
    query_one = query_units([side3], [theirs[3]], gain, query_weight, state, tables)
    return (updated[None], query_one[None])


def solution(mesh):
    in_specs = (
        P(("groups", "replica"), "tensor", None),
        P("tensor", None),
        P(("groups", "replica"), "tensor", None, None),
        P(),
        P("tensor", None),
        P(("groups", "replica")),
        P(("groups", "replica"), None),
    )
    out_specs = (
        P(("groups", "replica"), "tensor", None, None),
        P(("groups", "replica"), "tensor", None),
    )
    local = local_eight if mesh.shape["tensor"] == 8 and mesh.shape["replica"] == 2 else local_general
    return jax.shard_map(local, mesh=mesh, in_specs=in_specs, out_specs=out_specs, check_vma=False)
```

```python
import functools
import math

import jax
import jax.numpy as jnp
from jax import lax
from jax.experimental import pallas as pl
from jax.experimental.pallas import tpu as pltpu
from jax.sharding import PartitionSpec as P

HEAD = 128
HB = 128


eps_norm = 1e-05
eps_scale = 1e-06
code_top = 448.0
least_normal = 0.015625
rope_base = 500000.0

bf16 = jnp.bfloat16
f32 = jnp.float32


def hadamard_table(order_size):
    row_ids = lax.broadcasted_iota(jnp.int32, (order_size, order_size), 0)
    col_ids = lax.broadcasted_iota(jnp.int32, (order_size, order_size), 1)
    common = jnp.bitwise_and(row_ids, col_ids)
    parity = jnp.zeros((order_size, order_size), jnp.int32)
    for shift_bits in range(order_size.bit_length()):
        parity = parity + jnp.bitwise_and(jnp.right_shift(common, shift_bits), 1)
    sign_table = (1 - 2 * (parity % 2)).astype(jnp.float32)
    return sign_table / math.sqrt(order_size)


def hadamard_signs():
    row_ids = lax.broadcasted_iota(jnp.int32, (2 * HB, HB), 0)
    col_ids = lax.broadcasted_iota(jnp.int32, (2 * HB, HB), 1)
    common = jnp.bitwise_and(row_ids, col_ids)
    for shift_bits in (4, 2, 1):
        common = jnp.bitwise_xor(common, jnp.right_shift(common, shift_bits))
    return (1 - 2 * jnp.bitwise_and(common, 1)).astype(f32).astype(bf16)


def grid_code(scaled):
    magnitude = jnp.maximum(jnp.abs(scaled), least_normal)
    binade = jnp.floor(jnp.log2(magnitude))
    spacing = jnp.exp2(binade - 3.0)
    return spacing * jnp.floor(scaled / spacing + 0.5)


def positions_of(prefix_one, length_row, token_count):
    seg_total = length_row.shape[0]
    before = lax.broadcasted_iota(jnp.int32, (seg_total, seg_total), 0) < lax.broadcasted_iota(
        jnp.int32, (seg_total, seg_total), 1
    )
    seg_starts = jnp.sum(jnp.where(before, length_row[:, None], 0), axis=0)
    token_place = lax.broadcasted_iota(jnp.int32, (token_count, seg_total), 0)
    started = token_place >= seg_starts[None, :]
    seg_start = jnp.max(jnp.where(started, seg_starts[None, :], 0), axis=1)
    return (prefix_one + token_place[:, 0] - seg_start).astype(jnp.float32)


def rotate_rows(projected, columns, positions):
    token_count = projected.shape[1]
    even_columns = columns.reshape(-1, 2)[:, 0]
    pair_index = even_columns % HEAD // 2
    inv_freq = jnp.exp(pair_index.astype(jnp.float32) * (-2.0 * math.log(rope_base) / HEAD))
    angles = inv_freq[:, None] * positions[None, :]
    cosine = jnp.cos(angles)
    sine_part = jnp.sin(angles)
    paired = projected.reshape(-1, 2, token_count)
    even_part = paired[:, 0]
    odd_part = paired[:, 1]
    rotated_pairs = jnp.stack(
        [even_part * cosine - odd_part * sine_part, even_part * sine_part + odd_part * cosine],
        axis=1,
    )
    return rotated_pairs.reshape(projected.shape)


def local_general(hidden, down_weight, residual, norm_gain, query_weight, prefix_len, seg_lengths):
    members = lax.axis_size("tensor")
    span_len = hidden.shape[2]
    model_width = down_weight.shape[1]
    blocks = model_width // HB
    splits = max(1, members // blocks)
    piece_len = span_len // splits
    item_total = splits * blocks
    per_device = item_total // members
    hadamard = hadamard_table(HB)
    partial_value = lax.dot_general(
        hidden[0], down_weight, (((0,), (0,)), ((), ())), preferred_element_type=jnp.float32
    )
    partial_value = partial_value.reshape(splits, piece_len, blocks, HB).transpose(0, 2, 1, 3)
    rotated = jnp.einsum("sbch,hk->sbck", partial_value, hadamard, precision=lax.Precision.HIGHEST)
    block_scale = (jnp.max(jnp.abs(rotated), axis=3, keepdims=True) + eps_scale) / code_top
    block_code = grid_code(rotated / block_scale).astype(jnp.bfloat16)
    sent_codes = block_code.reshape(members, per_device, piece_len, HB)
    sent_scales = block_scale.reshape(members, per_device, piece_len)
    got_codes = lax.all_to_all(sent_codes, "tensor", split_axis=0, concat_axis=0, tiled=True)
    got_scales = lax.all_to_all(
        sent_scales.astype(jnp.bfloat16), "tensor", split_axis=0, concat_axis=0, tiled=True
    ).astype(sent_scales.dtype)
    running = jnp.sum(got_codes.astype(jnp.float32) * got_scales[..., None], axis=0)
    item_count = running.shape[0]
    unrotated = jnp.dot(running.reshape(-1, HB), hadamard, precision=lax.Precision.HIGHEST)
    restored = unrotated.reshape(item_count, piece_len, HB)
    updated = (residual[0].astype(jnp.float32) + restored).astype(jnp.bfloat16)
    gathered = lax.all_gather(updated, "tensor", axis=0, tiled=True)
    widened = gathered.astype(jnp.float32).reshape(splits, blocks, piece_len, HB)
    mean_square = jnp.mean(widened * widened, axis=(1, 3), keepdims=True)
    gain_blocks = norm_gain.reshape(1, blocks, 1, HB)
    normed = (widened * lax.rsqrt(mean_square + eps_norm) * gain_blocks).astype(jnp.bfloat16)
    column_count = query_weight.shape[0]
    weight_blocks = query_weight.reshape(column_count, blocks, HB)
    projected = jnp.einsum(
        "qbh,sbch->qsc", weight_blocks, normed, preferred_element_type=jnp.float32
    ).reshape(column_count, span_len)
    positions = positions_of(prefix_len[0], seg_lengths[0], span_len)
    columns = lax.axis_index("tensor") * column_count + lax.iota(jnp.int32, column_count)
    query_one = rotate_rows(projected, columns, positions).astype(jnp.bfloat16)
    return (updated[None], query_one[None])


def split_dot(value, signs):
    high = value.astype(bf16)
    low = (value - high.astype(f32)).astype(bf16)
    return jnp.dot(jnp.concatenate([high, low], axis=1), signs, preferred_element_type=f32)


def coded(total, signs):
    for j in range(total.shape[1] // HB):
        rotated = split_dot(total[:, j * HB : (j + 1) * HB], signs)
        top = jnp.max(jnp.abs(rotated), axis=1, keepdims=True) * (1.0 / math.sqrt(HB)) + eps_scale
        scaled = rotated * ((code_top / math.sqrt(HB)) / top)
        anchor = jnp.maximum(jnp.abs(scaled), least_normal) * (2.0**20 - 4.0)
        code = (scaled + anchor) - anchor
        yield code * (top * (1.0 / code_top))


def next_fetches(weight_ref, units, places, outs, sems):
    width = outs[0].shape[1]
    return [
        pltpu.make_async_copy(
            weight_ref.at[:, pl.ds(pl.multiple_of(units[p] * width, width), width)], out, sems.at[k]
        )
        for k, (p, out) in enumerate(zip(places, outs))
    ]


def down_kernel(count, first, later, chunk, units, *refs):
    if later:
        *refs, ahead, held, sems, ahead_sems = refs
        query_ref, *refs = refs
        refs = [*refs, held, sems]
    if first:
        rows_ref, weight_ref, out, turned, signs_out, held, sems, held_rows, row_sem = refs
        outs = [out]
    else:
        rows_ref, weight_ref, signs_ref, *outs, held, sems = refs
    depth, width = held.shape[1:]
    chunks = depth // chunk

    def fetch(k, c):
        here = pl.ds(c * chunk, chunk)
        columns = pl.ds(pl.multiple_of(units[k] * width, width), width)
        return pltpu.make_async_copy(weight_ref.at[here, columns], held.at[k, here], sems.at[k, c])

    if first:
        bring = pltpu.make_async_copy(rows_ref, held_rows, row_sem)
        bring.start()
    for k in range(count):
        for c in range(chunks):
            fetch(k, c).start()
    coming = next_fetches(query_ref, units, [count], [ahead], ahead_sems) if later else []
    for copy in coming:
        copy.start()
    if first:
        signs = hadamard_signs()
        signs_out[...] = signs
        bring.wait()
    else:
        signs = signs_ref[...]
    for k in range(count):
        total = None
        for c in range(chunks):
            here = slice(c * chunk, (c + 1) * chunk)
            if first:
                rows = held_rows[here, :].T
                turned[:, here] = rows
            else:
                rows = rows_ref[:, here]
            fetch(k, c).wait()
            product = jnp.dot(rows, held[k, here, :], preferred_element_type=f32)
            total = product if total is None else total + product
        for j, value in enumerate(coded(total, signs)):
            outs[k][j] = value.astype(outs[k].dtype)
    for copy in coming:
        copy.wait()


def down_units(rows, down_weight, signs, units, dtypes, query_weight=None, later=None):
    count = len(dtypes)
    first = signs is None
    tokens, depth = rows.shape[::-1] if first else rows.shape
    unit_width = down_weight.shape[1] // 8
    chunk = 512 if depth % 512 == 0 else depth
    vmem = pl.BlockSpec(memory_space=pltpu.VMEM)
    hbm = pl.BlockSpec(memory_space=pltpu.HBM)
    out_shape = [jax.ShapeDtypeStruct((unit_width // HB, tokens, HB), d) for d in dtypes]
    scratch = [
        pltpu.VMEM((count, depth, unit_width), bf16),
        pltpu.SemaphoreType.DMA((count, depth // chunk)),
    ]
    if first:
        out_shape.append(jax.ShapeDtypeStruct((tokens, depth), bf16))
        out_shape.append(jax.ShapeDtypeStruct((2 * HB, HB), bf16))
        scratch += [pltpu.VMEM((depth, tokens), bf16), pltpu.SemaphoreType.DMA]
        args, in_specs = (rows, down_weight), [hbm, hbm]
    else:
        args, in_specs = (rows, down_weight, signs), [vmem, hbm, vmem]
    if later is not None:
        args, in_specs = (query_weight, *args), [hbm, *in_specs]
        units = [*units, later]
        out_shape.append(jax.ShapeDtypeStruct((query_weight.shape[0], unit_width), bf16))
        scratch.append(pltpu.SemaphoreType.DMA((1,)))
    return pl.pallas_call(
        functools.partial(down_kernel, count, first, later is not None, chunk),
        in_specs=[pl.BlockSpec(memory_space=pltpu.SMEM), *in_specs],
        out_specs=[vmem] * len(out_shape),
        out_shape=out_shape,
        scratch_shapes=scratch,
        compiler_params=pltpu.CompilerParams(vmem_limit_bytes=(48 if first or later is not None else 32) << 20),
        cost_estimate=pl.CostEstimate(
            flops=2 * tokens * depth * unit_width * count,
            bytes_accessed=2 * depth * unit_width * count,
            transcendentals=0,
        ),
        name="down_units",
    )(jnp.stack(units), *args)


def update_kernel(own_ref, *refs):
    *terms, residual_ref, signs_ref, out_ref, turned_ref = refs
    signs = signs_ref[...]
    for j in range(own_ref.shape[0]):
        summed = own_ref[j]
        for term in terms:
            summed = summed + term[j].astype(f32)
        restored = split_dot(summed, signs) * (1.0 / math.sqrt(HB))
        value = (residual_ref[j].astype(f32) + restored).astype(out_ref.dtype)
        out_ref[j] = value
        turned_ref[j] = value.T


def update(own, terms, residual, signs):
    vmem = pl.BlockSpec(memory_space=pltpu.VMEM)
    blocks, tokens, _ = residual.shape
    return pl.pallas_call(
        update_kernel,
        in_specs=[vmem] * (len(terms) + 3),
        out_specs=[vmem, vmem],
        out_shape=[
            jax.ShapeDtypeStruct(residual.shape, residual.dtype),
            jax.ShapeDtypeStruct((blocks, HB, tokens), residual.dtype),
        ],
        compiler_params=pltpu.CompilerParams(vmem_limit_bytes=24 << 20),
        name="update",
    )(own, *terms, residual, signs)


def query_kernel(info, units, *refs):
    count, chunk, first, last, following = (info[n] for n in ("count", "chunk", "first", "last", "following"))
    refs = list(refs)
    streams = [refs.pop(0) for _ in range(count)]
    gain_ref = refs.pop(0)
    now = [refs.pop(0) for _ in range(count)]
    if not last:
        weight_ref = refs.pop(0)
    if not first:
        acc_in, square_in = refs.pop(0), refs.pop(0)
    if last:
        cos_ref, sin_ref, out_ref = refs
    else:
        acc_ref, square_ref, *ahead, sems = refs
        coming = next_fetches(weight_ref, units, range(count, count + following), ahead, sems)
        for copy in coming:
            copy.start()
    blocks, _, tokens = streams[0].shape
    width = blocks * HB
    chunks = now[0].shape[0] // chunk
    squares = None if first else square_in[...]
    factors = []
    for k in range(count):
        parts = []
        gains = gain_ref[pl.ds(pl.multiple_of(units[k] * blocks, blocks), blocks), :].T
        for j in range(blocks):
            value = streams[k][j].astype(f32)
            squares = value * value if squares is None else squares + value * value
            parts.append((value * gains[:, j : j + 1]).astype(bf16))
        factors.append(jnp.concatenate(parts, axis=0))
    if last:
        mean_square = jnp.sum(squares, axis=0, keepdims=True) * (1.0 / info["width"])
        root = lax.rsqrt(mean_square + eps_norm)
        even = lax.broadcasted_iota(jnp.int32, (HEAD, tokens), 0) % 2 == 0
    else:
        square_ref[...] = squares
    for c in range(chunks):
        here = slice(c * chunk, (c + 1) * chunk)
        total = None if first else acc_in[here, :]
        for k in range(count):
            product = jnp.dot(now[k][here, :], factors[k], preferred_element_type=f32)
            total = product if total is None else total + product
        if not last:
            acc_ref[here, :] = total
            continue
        for h in range(chunk // HEAD):
            value = total[h * HEAD : (h + 1) * HEAD, :] * root
            other = jnp.where(even, pltpu.roll(value, HEAD - 1, 0), pltpu.roll(value, 1, 0))
            rotated = value * cos_ref[...] + other * sin_ref[...]
            out_ref[c * chunk + h * HEAD : c * chunk + (h + 1) * HEAD, :] = rotated.astype(out_ref.dtype)
    if not last:
        for copy in coming:
            copy.wait()


def query_units(streams, units, later, gain, query_weight, ahead, carried=None, tables=None):
    count, following = len(streams), len(later)
    blocks, _, tokens = streams[0].shape
    columns, width = query_weight.shape
    unit_width = blocks * HB
    first, last = carried is None, tables is not None
    info = dict(count=count, chunk=512, first=first, last=last, following=following, width=width)
    vmem = pl.BlockSpec(memory_space=pltpu.VMEM)
    args = [jnp.stack([*units, *later]), *streams, gain, *ahead]
    in_specs = [pl.BlockSpec(memory_space=pltpu.SMEM)] + [vmem] * (2 * count + 1)
    if not last:
        args.append(query_weight)
        in_specs.append(pl.BlockSpec(memory_space=pltpu.HBM))
    rest = [*(carried or ()), *(tables or ())]
    if last:
        out_shape, scratch = [jax.ShapeDtypeStruct((columns, tokens), bf16)], []
    else:
        out_shape = [
            jax.ShapeDtypeStruct((columns, tokens), f32),
            jax.ShapeDtypeStruct((HB, tokens), f32),
        ]
        out_shape += [jax.ShapeDtypeStruct((columns, unit_width), bf16)] * following
        scratch = [pltpu.SemaphoreType.DMA((following,))]
    return pl.pallas_call(
        functools.partial(query_kernel, info),
        in_specs=in_specs + [vmem] * len(rest),
        out_specs=[vmem] * len(out_shape),
        out_shape=out_shape,
        scratch_shapes=scratch,
        compiler_params=pltpu.CompilerParams(vmem_limit_bytes=42 << 20),
        cost_estimate=pl.CostEstimate(
            flops=2 * tokens * columns * unit_width * count,
            bytes_accessed=2 * columns * unit_width * count,
            transcendentals=0,
        ),
        name="query_units",
    )(*args, *rest)


def rotary_tables(positions):
    row_ids = jnp.arange(HEAD, dtype=jnp.int32)
    inv_freq = jnp.exp((row_ids // 2).astype(f32) * (-2.0 * math.log(rope_base) / HEAD))
    angles = inv_freq[:, None] * positions[None, :]
    sign = jnp.where(row_ids % 2 == 0, -1.0, 1.0).astype(f32)
    return jnp.cos(angles), jnp.sin(angles) * sign[:, None]


def pairs_of(partner):
    found = []
    for z in range(4):
        for x in range(2):
            for core in range(2):
                pz, px, pcore = partner(z, x, core)
                found.append(((2 * z + x) * 2 + core, (2 * pz + px) * 2 + pcore))
    return found


ACROSS = pairs_of(lambda z, x, core: (z, 1 - x, core))
TWINS = pairs_of(lambda z, x, core: (z ^ 1, x, core))
MIDDLE = pairs_of(lambda z, x, core: (3 - z, x, core) if z in (1, 2) else (z, x, 1 - core))


def after(*values):
    return lax.optimization_barrier(values)


def send(value, pairs):
    return lax.ppermute(value.astype(bf16), ("tensor", "replica"), pairs)


def local_eight(hidden, down_weight, residual, norm_gain, query_weight, prefix_len, seg_lengths):
    place = lax.axis_index("tensor").astype(jnp.int32)
    z, x = place // 2, place % 2
    tokens = hidden.shape[2]
    slot = [z, z ^ 1, jnp.where(z < 2, 2, 1), jnp.where(z < 2, 3, 0)]
    mine = [2 * s + x for s in slot]
    theirs = [2 * s + 1 - x for s in slot]
    inner = (z == 1) | (z == 2)

    def down(units, dtypes, rows):
        return down_units(rows, down_weight, signs, units, dtypes)

    def only(here, value):
        return jnp.where(here, value, jnp.zeros_like(value))

    out3, rows, signs = down_units(hidden[0], down_weight, None, [theirs[3]], [bf16])
    got3 = send(out3, ACROSS)
    own3, out2 = down([mine[3], theirs[2]], [f32, bf16], rows)
    got2 = send(out2, ACROSS)
    part3, rows = after((own3 + got3).astype(bf16), rows)
    add3 = only(inner, send(part3, TWINS))
    own2, out1 = down([mine[2], theirs[1]], [f32, bf16], rows)
    got1 = send(out1, ACROSS)
    part2 = (own2 + got2).astype(bf16)
    add2 = only(inner, send(part2, TWINS))
    part3 = (own3 + got3 + add3).astype(bf16)
    part2, part3, rows = after(part2, part3, rows)
    add1 = only(inner, send(part3, MIDDLE))
    own1, out0 = down([mine[1], theirs[0]], [f32, bf16], rows)
    got0 = send(out0, ACROSS)
    part1 = (own1 + got1 + add1).astype(bf16)
    part2 = only(inner, (own2 + got2 + add2).astype(bf16))
    part1, part2, rows = after(part1, part2, rows)
    from1 = send(part1, TWINS)
    from2 = send(part2, MIDDLE)
    own0, *ahead = down_units(rows, down_weight, signs, [mine[0]], [f32], query_weight, mine[0])
    updated, unit0 = update(own0, [got0, from2, from1], residual[0], signs)

    gain = norm_gain.reshape(-1, HB)
    tables = rotary_tables(positions_of(prefix_len[0], seg_lengths[0], tokens))

    def query(streams, units, later, ahead, state=None):
        acc, square, *ahead = query_units(streams, units, later, gain, query_weight, ahead, state)
        return (acc, square), ahead

    side0 = send(unit0, ACROSS)
    unit1 = send(unit0, TWINS)
    inner2 = send(unit0, MIDDLE)
    state, ahead = query([unit0], [mine[0]], [theirs[0], mine[1]], ahead)
    unit1, state = after(unit1, state)
    side1 = send(unit1, ACROSS)
    inner3 = send(unit1, MIDDLE)
    unit2 = jnp.where(inner, inner2, send(inner2, TWINS))
    state, ahead = query([side0, unit1], [theirs[0], mine[1]], [theirs[1], mine[2]], ahead, state)
    inner3, state = after(inner3, state)
    unit3 = jnp.where(inner, inner3, send(inner3, TWINS))
    side2 = send(unit2, ACROSS)
    state, ahead = query([side1, unit2], [theirs[1], mine[2]], [theirs[2], mine[3]], ahead, state)
    unit3, state = after(unit3, state)
    side3 = send(unit3, ACROSS)
    state, ahead = query([side2, unit3], [theirs[2], mine[3]], [theirs[3]], ahead, state)
    query_one, = query_units([side3], [theirs[3]], [], gain, query_weight, ahead, state, tables)
    return (updated[None], query_one[None])


def solution(mesh):
    in_specs = (
        P(("groups", "replica"), "tensor", None),
        P("tensor", None),
        P(("groups", "replica"), "tensor", None, None),
        P(),
        P("tensor", None),
        P(("groups", "replica")),
        P(("groups", "replica"), None),
    )
    out_specs = (
        P(("groups", "replica"), "tensor", None, None),
        P(("groups", "replica"), "tensor", None),
    )
    local = local_eight if mesh.shape["tensor"] == 8 and mesh.shape["replica"] == 2 else local_general
    return jax.shard_map(local, mesh=mesh, in_specs=in_specs, out_specs=out_specs, check_vma=False)
```

```python
import functools
import math

import jax
import jax.numpy as jnp
from jax import lax
from jax.experimental import pallas as pl
from jax.experimental.pallas import tpu as pltpu
from jax.sharding import PartitionSpec as P

HEAD = 128
HB = 128


eps_norm = 1e-05
eps_scale = 1e-06
code_top = 448.0
least_normal = 0.015625
rope_base = 500000.0

bf16 = jnp.bfloat16
f32 = jnp.float32


def hadamard_table(order_size):
    row_ids = lax.broadcasted_iota(jnp.int32, (order_size, order_size), 0)
    col_ids = lax.broadcasted_iota(jnp.int32, (order_size, order_size), 1)
    common = jnp.bitwise_and(row_ids, col_ids)
    parity = jnp.zeros((order_size, order_size), jnp.int32)
    for shift_bits in range(order_size.bit_length()):
        parity = parity + jnp.bitwise_and(jnp.right_shift(common, shift_bits), 1)
    sign_table = (1 - 2 * (parity % 2)).astype(jnp.float32)
    return sign_table / math.sqrt(order_size)


def hadamard_signs():
    row_ids = lax.broadcasted_iota(jnp.int32, (2 * HB, HB), 0)
    col_ids = lax.broadcasted_iota(jnp.int32, (2 * HB, HB), 1)
    common = jnp.bitwise_and(row_ids, col_ids)
    for shift_bits in (4, 2, 1):
        common = jnp.bitwise_xor(common, jnp.right_shift(common, shift_bits))
    return (1 - 2 * jnp.bitwise_and(common, 1)).astype(f32).astype(bf16)


def grid_code(scaled):
    magnitude = jnp.maximum(jnp.abs(scaled), least_normal)
    binade = jnp.floor(jnp.log2(magnitude))
    spacing = jnp.exp2(binade - 3.0)
    return spacing * jnp.floor(scaled / spacing + 0.5)


def positions_of(prefix_one, length_row, token_count):
    seg_total = length_row.shape[0]
    before = lax.broadcasted_iota(jnp.int32, (seg_total, seg_total), 0) < lax.broadcasted_iota(
        jnp.int32, (seg_total, seg_total), 1
    )
    seg_starts = jnp.sum(jnp.where(before, length_row[:, None], 0), axis=0)
    token_place = lax.broadcasted_iota(jnp.int32, (token_count, seg_total), 0)
    started = token_place >= seg_starts[None, :]
    seg_start = jnp.max(jnp.where(started, seg_starts[None, :], 0), axis=1)
    return (prefix_one + token_place[:, 0] - seg_start).astype(jnp.float32)


def rotate_rows(projected, columns, positions):
    token_count = projected.shape[1]
    even_columns = columns.reshape(-1, 2)[:, 0]
    pair_index = even_columns % HEAD // 2
    inv_freq = jnp.exp(pair_index.astype(jnp.float32) * (-2.0 * math.log(rope_base) / HEAD))
    angles = inv_freq[:, None] * positions[None, :]
    cosine = jnp.cos(angles)
    sine_part = jnp.sin(angles)
    paired = projected.reshape(-1, 2, token_count)
    even_part = paired[:, 0]
    odd_part = paired[:, 1]
    rotated_pairs = jnp.stack(
        [even_part * cosine - odd_part * sine_part, even_part * sine_part + odd_part * cosine],
        axis=1,
    )
    return rotated_pairs.reshape(projected.shape)


def local_general(hidden, down_weight, residual, norm_gain, query_weight, prefix_len, seg_lengths):
    members = lax.axis_size("tensor")
    span_len = hidden.shape[2]
    model_width = down_weight.shape[1]
    blocks = model_width // HB
    splits = max(1, members // blocks)
    piece_len = span_len // splits
    item_total = splits * blocks
    per_device = item_total // members
    hadamard = hadamard_table(HB)
    partial_value = lax.dot_general(
        hidden[0], down_weight, (((0,), (0,)), ((), ())), preferred_element_type=jnp.float32
    )
    partial_value = partial_value.reshape(splits, piece_len, blocks, HB).transpose(0, 2, 1, 3)
    rotated = jnp.einsum("sbch,hk->sbck", partial_value, hadamard, precision=lax.Precision.HIGHEST)
    block_scale = (jnp.max(jnp.abs(rotated), axis=3, keepdims=True) + eps_scale) / code_top
    block_code = grid_code(rotated / block_scale).astype(jnp.bfloat16)
    sent_codes = block_code.reshape(members, per_device, piece_len, HB)
    sent_scales = block_scale.reshape(members, per_device, piece_len)
    got_codes = lax.all_to_all(sent_codes, "tensor", split_axis=0, concat_axis=0, tiled=True)
    got_scales = lax.all_to_all(
        sent_scales.astype(jnp.bfloat16), "tensor", split_axis=0, concat_axis=0, tiled=True
    ).astype(sent_scales.dtype)
    running = jnp.sum(got_codes.astype(jnp.float32) * got_scales[..., None], axis=0)
    item_count = running.shape[0]
    unrotated = jnp.dot(running.reshape(-1, HB), hadamard, precision=lax.Precision.HIGHEST)
    restored = unrotated.reshape(item_count, piece_len, HB)
    updated = (residual[0].astype(jnp.float32) + restored).astype(jnp.bfloat16)
    gathered = lax.all_gather(updated, "tensor", axis=0, tiled=True)
    widened = gathered.astype(jnp.float32).reshape(splits, blocks, piece_len, HB)
    mean_square = jnp.mean(widened * widened, axis=(1, 3), keepdims=True)
    gain_blocks = norm_gain.reshape(1, blocks, 1, HB)
    normed = (widened * lax.rsqrt(mean_square + eps_norm) * gain_blocks).astype(jnp.bfloat16)
    column_count = query_weight.shape[0]
    weight_blocks = query_weight.reshape(column_count, blocks, HB)
    projected = jnp.einsum(
        "qbh,sbch->qsc", weight_blocks, normed, preferred_element_type=jnp.float32
    ).reshape(column_count, span_len)
    positions = positions_of(prefix_len[0], seg_lengths[0], span_len)
    columns = lax.axis_index("tensor") * column_count + lax.iota(jnp.int32, column_count)
    query_one = rotate_rows(projected, columns, positions).astype(jnp.bfloat16)
    return (updated[None], query_one[None])


def split_dot(value, signs):
    high = value.astype(bf16)
    low = (value - high.astype(f32)).astype(bf16)
    return jnp.dot(jnp.concatenate([high, low], axis=1), signs, preferred_element_type=f32)


def coded(total, signs):
    for j in range(total.shape[1] // HB):
        rotated = split_dot(total[:, j * HB : (j + 1) * HB], signs)
        top = jnp.max(jnp.abs(rotated), axis=1, keepdims=True) * (1.0 / math.sqrt(HB)) + eps_scale
        scaled = rotated * ((code_top / math.sqrt(HB)) / top)
        anchor = jnp.maximum(jnp.abs(scaled), least_normal) * (2.0**20 - 4.0)
        code = (scaled + anchor) - anchor
        yield code * (top * (1.0 / code_top))


def next_fetches(weight_ref, units, places, outs, sems):
    width = outs[0].shape[1]
    return [
        pltpu.make_async_copy(
            weight_ref.at[:, pl.ds(pl.multiple_of(units[p] * width, width), width)], out, sems.at[k]
        )
        for k, (p, out) in enumerate(zip(places, outs))
    ]


def down_kernel(count, first, later, chunk, units, *refs):
    if later:
        query_ref, *refs, held, sems, ahead_sems = refs
        ahead = refs[-later:]
        refs = [*refs[:-later], held, sems]
    if first:
        rows_ref, weight_ref, out, turned, signs_out, held, sems, held_rows, row_sem = refs
        outs = [out]
    else:
        rows_ref, weight_ref, signs_ref, *outs, held, sems = refs
    depth, width = held.shape[1:]
    chunks = depth // chunk

    def fetch(k, c):
        here = pl.ds(c * chunk, chunk)
        columns = pl.ds(pl.multiple_of(units[k] * width, width), width)
        return pltpu.make_async_copy(weight_ref.at[here, columns], held.at[k, here], sems.at[k, c])

    if first:
        bring = pltpu.make_async_copy(rows_ref, held_rows, row_sem)
        bring.start()
    for k in range(count):
        for c in range(chunks):
            fetch(k, c).start()
    coming = next_fetches(query_ref, units, range(count, count + later), ahead, ahead_sems) if later else []
    for copy in coming:
        copy.start()
    if first:
        signs = hadamard_signs()
        signs_out[...] = signs
        bring.wait()
    else:
        signs = signs_ref[...]
    for k in range(count):
        total = None
        for c in range(chunks):
            here = slice(c * chunk, (c + 1) * chunk)
            if first:
                rows = held_rows[here, :].T
                turned[:, here] = rows
            else:
                rows = rows_ref[:, here]
            fetch(k, c).wait()
            product = jnp.dot(rows, held[k, here, :], preferred_element_type=f32)
            total = product if total is None else total + product
        for j, value in enumerate(coded(total, signs)):
            outs[k][j] = value.astype(outs[k].dtype)
    for copy in coming:
        copy.wait()


def down_units(rows, down_weight, signs, units, dtypes, query_weight=None, later=()):
    count = len(dtypes)
    first = signs is None
    tokens, depth = rows.shape[::-1] if first else rows.shape
    unit_width = down_weight.shape[1] // 8
    chunk = 512 if depth % 512 == 0 else depth
    vmem = pl.BlockSpec(memory_space=pltpu.VMEM)
    hbm = pl.BlockSpec(memory_space=pltpu.HBM)
    out_shape = [jax.ShapeDtypeStruct((unit_width // HB, tokens, HB), d) for d in dtypes]
    scratch = [
        pltpu.VMEM((count, depth, unit_width), bf16),
        pltpu.SemaphoreType.DMA((count, depth // chunk)),
    ]
    if first:
        out_shape.append(jax.ShapeDtypeStruct((tokens, depth), bf16))
        out_shape.append(jax.ShapeDtypeStruct((2 * HB, HB), bf16))
        scratch += [pltpu.VMEM((depth, tokens), bf16), pltpu.SemaphoreType.DMA]
        args, in_specs = (rows, down_weight), [hbm, hbm]
    else:
        args, in_specs = (rows, down_weight, signs), [vmem, hbm, vmem]
    if later:
        args, in_specs = (query_weight, *args), [hbm, *in_specs]
        units = [*units, *later]
        out_shape += [jax.ShapeDtypeStruct((query_weight.shape[0], unit_width), bf16)] * len(later)
        scratch.append(pltpu.SemaphoreType.DMA((len(later),)))
    return pl.pallas_call(
        functools.partial(down_kernel, count, first, len(later), chunk),
        in_specs=[pl.BlockSpec(memory_space=pltpu.SMEM), *in_specs],
        out_specs=[vmem] * len(out_shape),
        out_shape=out_shape,
        scratch_shapes=scratch,
        compiler_params=pltpu.CompilerParams(vmem_limit_bytes=(48 if first or later else 32) << 20),
        cost_estimate=pl.CostEstimate(
            flops=2 * tokens * depth * unit_width * count,
            bytes_accessed=2 * depth * unit_width * count,
            transcendentals=0,
        ),
        name="down_units",
    )(jnp.stack(units), *args)


def update_kernel(own_ref, *refs):
    *terms, residual_ref, signs_ref, out_ref, turned_ref = refs
    signs = signs_ref[...]
    for j in range(own_ref.shape[0]):
        summed = own_ref[j]
        for term in terms:
            summed = summed + term[j].astype(f32)
        restored = split_dot(summed, signs) * (1.0 / math.sqrt(HB))
        value = (residual_ref[j].astype(f32) + restored).astype(out_ref.dtype)
        out_ref[j] = value
        turned_ref[j] = value.T


def update(own, terms, residual, signs):
    vmem = pl.BlockSpec(memory_space=pltpu.VMEM)
    blocks, tokens, _ = residual.shape
    return pl.pallas_call(
        update_kernel,
        in_specs=[vmem] * (len(terms) + 3),
        out_specs=[vmem, vmem],
        out_shape=[
            jax.ShapeDtypeStruct(residual.shape, residual.dtype),
            jax.ShapeDtypeStruct((blocks, HB, tokens), residual.dtype),
        ],
        compiler_params=pltpu.CompilerParams(vmem_limit_bytes=24 << 20),
        name="update",
    )(own, *terms, residual, signs)


def query_kernel(info, units, *refs):
    count, chunk, first, last, following = (info[n] for n in ("count", "chunk", "first", "last", "following"))
    refs = list(refs)
    streams = [refs.pop(0) for _ in range(count)]
    gain_ref = refs.pop(0)
    now = [refs.pop(0) for _ in range(count)]
    if not last:
        weight_ref = refs.pop(0)
    if not first:
        acc_in, square_in = refs.pop(0), refs.pop(0)
    if last:
        cos_ref, sin_ref, out_ref = refs
    else:
        acc_ref, square_ref, *ahead, sems = refs
        coming = next_fetches(weight_ref, units, range(count, count + following), ahead, sems)
        for copy in coming:
            copy.start()
    blocks, _, tokens = streams[0].shape
    width = blocks * HB
    chunks = now[0].shape[0] // chunk
    squares = None if first else square_in[...]
    factors = []
    for k in range(count):
        parts = []
        gains = gain_ref[pl.ds(pl.multiple_of(units[k] * blocks, blocks), blocks), :].T
        for j in range(blocks):
            value = streams[k][j].astype(f32)
            squares = value * value if squares is None else squares + value * value
            parts.append((value * gains[:, j : j + 1]).astype(bf16))
        factors.append(jnp.concatenate(parts, axis=0))
    if last:
        mean_square = jnp.sum(squares, axis=0, keepdims=True) * (1.0 / info["width"])
        root = lax.rsqrt(mean_square + eps_norm)
        even = lax.broadcasted_iota(jnp.int32, (HEAD, tokens), 0) % 2 == 0
    else:
        square_ref[...] = squares
    for c in range(chunks):
        here = slice(c * chunk, (c + 1) * chunk)
        total = None if first else acc_in[here, :]
        for k in range(count):
            product = jnp.dot(now[k][here, :], factors[k], preferred_element_type=f32)
            total = product if total is None else total + product
        if not last:
            acc_ref[here, :] = total
            continue
        for h in range(chunk // HEAD):
            value = total[h * HEAD : (h + 1) * HEAD, :] * root
            other = jnp.where(even, pltpu.roll(value, HEAD - 1, 0), pltpu.roll(value, 1, 0))
            rotated = value * cos_ref[...] + other * sin_ref[...]
            out_ref[c * chunk + h * HEAD : c * chunk + (h + 1) * HEAD, :] = rotated.astype(out_ref.dtype)
    if not last:
        for copy in coming:
            copy.wait()


def query_units(streams, units, later, gain, query_weight, ahead, carried=None, tables=None):
    count, following = len(streams), len(later)
    blocks, _, tokens = streams[0].shape
    columns, width = query_weight.shape
    unit_width = blocks * HB
    first, last = carried is None, tables is not None
    info = dict(count=count, chunk=512, first=first, last=last, following=following, width=width)
    vmem = pl.BlockSpec(memory_space=pltpu.VMEM)
    args = [jnp.stack([*units, *later]), *streams, gain, *ahead]
    in_specs = [pl.BlockSpec(memory_space=pltpu.SMEM)] + [vmem] * (2 * count + 1)
    if not last:
        args.append(query_weight)
        in_specs.append(pl.BlockSpec(memory_space=pltpu.HBM))
    rest = [*(carried or ()), *(tables or ())]
    if last:
        out_shape, scratch = [jax.ShapeDtypeStruct((columns, tokens), bf16)], []
    else:
        out_shape = [
            jax.ShapeDtypeStruct((columns, tokens), f32),
            jax.ShapeDtypeStruct((HB, tokens), f32),
        ]
        out_shape += [jax.ShapeDtypeStruct((columns, unit_width), bf16)] * following
        scratch = [pltpu.SemaphoreType.DMA((following,))]
    return pl.pallas_call(
        functools.partial(query_kernel, info),
        in_specs=in_specs + [vmem] * len(rest),
        out_specs=[vmem] * len(out_shape),
        out_shape=out_shape,
        scratch_shapes=scratch,
        compiler_params=pltpu.CompilerParams(vmem_limit_bytes=42 << 20),
        cost_estimate=pl.CostEstimate(
            flops=2 * tokens * columns * unit_width * count,
            bytes_accessed=2 * columns * unit_width * count,
            transcendentals=0,
        ),
        name="query_units",
    )(*args, *rest)


def rotary_tables(positions):
    row_ids = jnp.arange(HEAD, dtype=jnp.int32)
    inv_freq = jnp.exp((row_ids // 2).astype(f32) * (-2.0 * math.log(rope_base) / HEAD))
    angles = inv_freq[:, None] * positions[None, :]
    sign = jnp.where(row_ids % 2 == 0, -1.0, 1.0).astype(f32)
    return jnp.cos(angles), jnp.sin(angles) * sign[:, None]


def pairs_of(partner):
    found = []
    for z in range(4):
        for x in range(2):
            for core in range(2):
                pz, px, pcore = partner(z, x, core)
                found.append(((2 * z + x) * 2 + core, (2 * pz + px) * 2 + pcore))
    return found


ACROSS = pairs_of(lambda z, x, core: (z, 1 - x, core))
TWINS = pairs_of(lambda z, x, core: (z ^ 1, x, core))
MIDDLE = pairs_of(lambda z, x, core: (3 - z, x, core) if z in (1, 2) else (z, x, 1 - core))


def after(*values):
    return lax.optimization_barrier(values)


def send(value, pairs):
    return lax.ppermute(value.astype(bf16), ("tensor", "replica"), pairs)


def local_eight(hidden, down_weight, residual, norm_gain, query_weight, prefix_len, seg_lengths):
    place = lax.axis_index("tensor").astype(jnp.int32)
    z, x = place // 2, place % 2
    tokens = hidden.shape[2]
    slot = [z, z ^ 1, jnp.where(z < 2, 2, 1), jnp.where(z < 2, 3, 0)]
    mine = [2 * s + x for s in slot]
    theirs = [2 * s + 1 - x for s in slot]
    inner = (z == 1) | (z == 2)

    def down(units, dtypes, rows):
        return down_units(rows, down_weight, signs, units, dtypes)

    def only(here, value):
        return jnp.where(here, value, jnp.zeros_like(value))

    out3, rows, signs = down_units(hidden[0], down_weight, None, [theirs[3]], [bf16])
    got3 = send(out3, ACROSS)
    own3, out2 = down([mine[3], theirs[2]], [f32, bf16], rows)
    got2 = send(out2, ACROSS)
    part3, rows = after((own3 + got3).astype(bf16), rows)
    add3 = only(inner, send(part3, TWINS))
    own2, out1 = down([mine[2], theirs[1]], [f32, bf16], rows)
    got1 = send(out1, ACROSS)
    part2 = (own2 + got2).astype(bf16)
    add2 = only(inner, send(part2, TWINS))
    part3 = (own3 + got3 + add3).astype(bf16)
    part2, part3, rows = after(part2, part3, rows)
    add1 = only(inner, send(part3, MIDDLE))
    own1, out0 = down([mine[1], theirs[0]], [f32, bf16], rows)
    got0 = send(out0, ACROSS)
    part1 = (own1 + got1 + add1).astype(bf16)
    part2 = only(inner, (own2 + got2 + add2).astype(bf16))
    part1, part2, rows = after(part1, part2, rows)
    from1 = send(part1, TWINS)
    from2 = send(part2, MIDDLE)
    early = [mine[0], theirs[0]]
    own0, ahead0, held = down_units(rows, down_weight, signs, [mine[0]], [f32], query_weight, early)
    from2, got0, _ = after(from2, got0, from1)
    updated, unit0 = update(own0, [got0, from2, from1], residual[0], signs)

    gain = norm_gain.reshape(-1, HB)

    def query(streams, units, later, ahead, state=None):
        acc, square, *ahead = query_units(streams, units, later, gain, query_weight, ahead, state)
        return (acc, square), ahead

    side0 = send(unit0, ACROSS)
    unit1 = send(unit0, TWINS)
    inner2 = send(unit0, MIDDLE)
    state, ahead = query([unit0], [mine[0]], [mine[1]], [ahead0])
    unit1, state = after(unit1, state)
    inner2, _ = after(inner2, unit1)
    side1 = send(unit1, ACROSS)
    inner3 = send(unit1, MIDDLE)
    unit2 = jnp.where(inner, inner2, send(inner2, TWINS))
    state, ahead = query([side0, unit1], [theirs[0], mine[1]], [theirs[1], mine[2]], [held, *ahead], state)
    inner3, state = after(inner3, state)
    unit3 = jnp.where(inner, inner3, send(inner3, TWINS))
    side2 = send(unit2, ACROSS)
    state, ahead = query([side1, unit2], [theirs[1], mine[2]], [theirs[2], mine[3]], ahead, state)
    unit3, state = after(unit3, state)
    prefix, lengths, _ = after(prefix_len[0], seg_lengths[0], unit3)
    tables = rotary_tables(positions_of(prefix, lengths, tokens))
    side3 = send(unit3, ACROSS)
    state, ahead = query([side2, unit3], [theirs[2], mine[3]], [theirs[3]], ahead, state)
    query_one, = query_units([side3], [theirs[3]], [], gain, query_weight, ahead, state, tables)
    return (updated[None], query_one[None])


def solution(mesh):
    in_specs = (
        P(("groups", "replica"), "tensor", None),
        P("tensor", None),
        P(("groups", "replica"), "tensor", None, None),
        P(),
        P("tensor", None),
        P(("groups", "replica")),
        P(("groups", "replica"), None),
    )
    out_specs = (
        P(("groups", "replica"), "tensor", None, None),
        P(("groups", "replica"), "tensor", None),
    )
    local = local_eight if mesh.shape["tensor"] == 8 and mesh.shape["replica"] == 2 else local_general
    return jax.shard_map(local, mesh=mesh, in_specs=in_specs, out_specs=out_specs, check_vma=False)
```

```python
import functools
import math

import jax
import jax.numpy as jnp
from jax import lax
from jax.experimental import pallas as pl
from jax.experimental.pallas import tpu as pltpu
from jax.sharding import PartitionSpec as P

HEAD = 128
HB = 128


eps_norm = 1e-05
eps_scale = 1e-06
code_top = 448.0
least_normal = 0.015625
rope_base = 500000.0

bf16 = jnp.bfloat16
f32 = jnp.float32


def hadamard_table(order_size):
    row_ids = lax.broadcasted_iota(jnp.int32, (order_size, order_size), 0)
    col_ids = lax.broadcasted_iota(jnp.int32, (order_size, order_size), 1)
    common = jnp.bitwise_and(row_ids, col_ids)
    parity = jnp.zeros((order_size, order_size), jnp.int32)
    for shift_bits in range(order_size.bit_length()):
        parity = parity + jnp.bitwise_and(jnp.right_shift(common, shift_bits), 1)
    sign_table = (1 - 2 * (parity % 2)).astype(jnp.float32)
    return sign_table / math.sqrt(order_size)


def hadamard_signs():
    row_ids = lax.broadcasted_iota(jnp.int32, (2 * HB, HB), 0)
    col_ids = lax.broadcasted_iota(jnp.int32, (2 * HB, HB), 1)
    common = jnp.bitwise_and(row_ids, col_ids)
    for shift_bits in (4, 2, 1):
        common = jnp.bitwise_xor(common, jnp.right_shift(common, shift_bits))
    return (1 - 2 * jnp.bitwise_and(common, 1)).astype(f32).astype(bf16)


def grid_code(scaled):
    magnitude = jnp.maximum(jnp.abs(scaled), least_normal)
    binade = jnp.floor(jnp.log2(magnitude))
    spacing = jnp.exp2(binade - 3.0)
    return spacing * jnp.floor(scaled / spacing + 0.5)


def positions_of(prefix_one, length_row, token_count):
    seg_total = length_row.shape[0]
    before = lax.broadcasted_iota(jnp.int32, (seg_total, seg_total), 0) < lax.broadcasted_iota(
        jnp.int32, (seg_total, seg_total), 1
    )
    seg_starts = jnp.sum(jnp.where(before, length_row[:, None], 0), axis=0)
    token_place = lax.broadcasted_iota(jnp.int32, (token_count, seg_total), 0)
    started = token_place >= seg_starts[None, :]
    seg_start = jnp.max(jnp.where(started, seg_starts[None, :], 0), axis=1)
    return (prefix_one + token_place[:, 0] - seg_start).astype(jnp.float32)


def rotate_rows(projected, columns, positions):
    token_count = projected.shape[1]
    even_columns = columns.reshape(-1, 2)[:, 0]
    pair_index = even_columns % HEAD // 2
    inv_freq = jnp.exp(pair_index.astype(jnp.float32) * (-2.0 * math.log(rope_base) / HEAD))
    angles = inv_freq[:, None] * positions[None, :]
    cosine = jnp.cos(angles)
    sine_part = jnp.sin(angles)
    paired = projected.reshape(-1, 2, token_count)
    even_part = paired[:, 0]
    odd_part = paired[:, 1]
    rotated_pairs = jnp.stack(
        [even_part * cosine - odd_part * sine_part, even_part * sine_part + odd_part * cosine],
        axis=1,
    )
    return rotated_pairs.reshape(projected.shape)


def local_general(hidden, down_weight, residual, norm_gain, query_weight, prefix_len, seg_lengths):
    members = lax.axis_size("tensor")
    span_len = hidden.shape[2]
    model_width = down_weight.shape[1]
    blocks = model_width // HB
    splits = max(1, members // blocks)
    piece_len = span_len // splits
    item_total = splits * blocks
    per_device = item_total // members
    hadamard = hadamard_table(HB)
    partial_value = lax.dot_general(
        hidden[0], down_weight, (((0,), (0,)), ((), ())), preferred_element_type=jnp.float32
    )
    partial_value = partial_value.reshape(splits, piece_len, blocks, HB).transpose(0, 2, 1, 3)
    rotated = jnp.einsum("sbch,hk->sbck", partial_value, hadamard, precision=lax.Precision.HIGHEST)
    block_scale = (jnp.max(jnp.abs(rotated), axis=3, keepdims=True) + eps_scale) / code_top
    block_code = grid_code(rotated / block_scale).astype(jnp.bfloat16)
    sent_codes = block_code.reshape(members, per_device, piece_len, HB)
    sent_scales = block_scale.reshape(members, per_device, piece_len)
    got_codes = lax.all_to_all(sent_codes, "tensor", split_axis=0, concat_axis=0, tiled=True)
    got_scales = lax.all_to_all(
        sent_scales.astype(jnp.bfloat16), "tensor", split_axis=0, concat_axis=0, tiled=True
    ).astype(sent_scales.dtype)
    running = jnp.sum(got_codes.astype(jnp.float32) * got_scales[..., None], axis=0)
    item_count = running.shape[0]
    unrotated = jnp.dot(running.reshape(-1, HB), hadamard, precision=lax.Precision.HIGHEST)
    restored = unrotated.reshape(item_count, piece_len, HB)
    updated = (residual[0].astype(jnp.float32) + restored).astype(jnp.bfloat16)
    gathered = lax.all_gather(updated, "tensor", axis=0, tiled=True)
    widened = gathered.astype(jnp.float32).reshape(splits, blocks, piece_len, HB)
    mean_square = jnp.mean(widened * widened, axis=(1, 3), keepdims=True)
    gain_blocks = norm_gain.reshape(1, blocks, 1, HB)
    normed = (widened * lax.rsqrt(mean_square + eps_norm) * gain_blocks).astype(jnp.bfloat16)
    column_count = query_weight.shape[0]
    weight_blocks = query_weight.reshape(column_count, blocks, HB)
    projected = jnp.einsum(
        "qbh,sbch->qsc", weight_blocks, normed, preferred_element_type=jnp.float32
    ).reshape(column_count, span_len)
    positions = positions_of(prefix_len[0], seg_lengths[0], span_len)
    columns = lax.axis_index("tensor") * column_count + lax.iota(jnp.int32, column_count)
    query_one = rotate_rows(projected, columns, positions).astype(jnp.bfloat16)
    return (updated[None], query_one[None])


def split_dot(value, signs):
    high = value.astype(bf16)
    low = (value - high.astype(f32)).astype(bf16)
    return jnp.dot(jnp.concatenate([high, low], axis=1), signs, preferred_element_type=f32)


def coded(total, signs):
    for j in range(total.shape[1] // HB):
        rotated = split_dot(total[:, j * HB : (j + 1) * HB], signs)
        top = jnp.max(jnp.abs(rotated), axis=1, keepdims=True) * (1.0 / math.sqrt(HB)) + eps_scale
        scaled = rotated * ((code_top / math.sqrt(HB)) / top)
        anchor = jnp.maximum(jnp.abs(scaled), least_normal) * (2.0**20 - 4.0)
        code = (scaled + anchor) - anchor
        yield code * (top * (1.0 / code_top))


def next_fetches(weight_ref, units, places, outs, sems):
    width = outs[0].shape[1]
    return [
        pltpu.make_async_copy(
            weight_ref.at[:, pl.ds(pl.multiple_of(units[p] * width, width), width)], out, sems.at[k]
        )
        for k, (p, out) in enumerate(zip(places, outs))
    ]


def down_kernel(count, first, later, chunk, units, *refs):
    if later:
        query_ref, *refs, held, sems, ahead_sems = refs
        ahead = refs[-later:]
        refs = [*refs[:-later], held, sems]
    if first:
        rows_ref, weight_ref, out, turned, signs_out, held, sems, held_rows, row_sem = refs
        outs = [out]
    else:
        rows_ref, weight_ref, signs_ref, *outs, held, sems = refs
    depth, width = held.shape[1:]
    chunks = depth // chunk

    def fetch(k, c):
        here = pl.ds(c * chunk, chunk)
        columns = pl.ds(pl.multiple_of(units[k] * width, width), width)
        return pltpu.make_async_copy(weight_ref.at[here, columns], held.at[k, here], sems.at[k, c])

    if first:
        bring = pltpu.make_async_copy(rows_ref, held_rows, row_sem)
        bring.start()
    for k in range(count):
        for c in range(chunks):
            fetch(k, c).start()
    coming = next_fetches(query_ref, units, range(count, count + later), ahead, ahead_sems) if later else []
    for copy in coming:
        copy.start()
    if first:
        signs = hadamard_signs()
        signs_out[...] = signs
        bring.wait()
    else:
        signs = signs_ref[...]
    for k in range(count):
        total = None
        for c in range(chunks):
            here = slice(c * chunk, (c + 1) * chunk)
            if first:
                rows = held_rows[here, :].T
                turned[:, here] = rows
            else:
                rows = rows_ref[:, here]
            fetch(k, c).wait()
            product = jnp.dot(rows, held[k, here, :], preferred_element_type=f32)
            total = product if total is None else total + product
        for j, value in enumerate(coded(total, signs)):
            outs[k][j] = value.astype(outs[k].dtype)
    for copy in coming:
        copy.wait()


def down_units(rows, down_weight, signs, units, dtypes, query_weight=None, later=()):
    count = len(dtypes)
    first = signs is None
    tokens, depth = rows.shape[::-1] if first else rows.shape
    unit_width = down_weight.shape[1] // 8
    chunk = 512 if depth % 512 == 0 else depth
    vmem = pl.BlockSpec(memory_space=pltpu.VMEM)
    hbm = pl.BlockSpec(memory_space=pltpu.HBM)
    out_shape = [jax.ShapeDtypeStruct((unit_width // HB, tokens, HB), d) for d in dtypes]
    scratch = [
        pltpu.VMEM((count, depth, unit_width), bf16),
        pltpu.SemaphoreType.DMA((count, depth // chunk)),
    ]
    if first:
        out_shape.append(jax.ShapeDtypeStruct((tokens, depth), bf16))
        out_shape.append(jax.ShapeDtypeStruct((2 * HB, HB), bf16))
        scratch += [pltpu.VMEM((depth, tokens), bf16), pltpu.SemaphoreType.DMA]
        args, in_specs = (rows, down_weight), [hbm, hbm]
    else:
        args, in_specs = (rows, down_weight, signs), [vmem, hbm, vmem]
    if later:
        args, in_specs = (query_weight, *args), [hbm, *in_specs]
        units = [*units, *later]
        out_shape += [jax.ShapeDtypeStruct((query_weight.shape[0], unit_width), bf16)] * len(later)
        scratch.append(pltpu.SemaphoreType.DMA((len(later),)))
    return pl.pallas_call(
        functools.partial(down_kernel, count, first, len(later), chunk),
        in_specs=[pl.BlockSpec(memory_space=pltpu.SMEM), *in_specs],
        out_specs=[vmem] * len(out_shape),
        out_shape=out_shape,
        scratch_shapes=scratch,
        compiler_params=pltpu.CompilerParams(vmem_limit_bytes=(48 if first or later else 32) << 20),
        cost_estimate=pl.CostEstimate(
            flops=2 * tokens * depth * unit_width * count,
            bytes_accessed=2 * depth * unit_width * count,
            transcendentals=0,
        ),
        name="down_units",
    )(jnp.stack(units), *args)


def update_kernel(own_ref, *refs):
    *terms, residual_ref, signs_ref, out_ref, turned_ref = refs
    signs = signs_ref[...]
    for j in range(own_ref.shape[0]):
        summed = own_ref[j]
        for term in terms:
            summed = summed + term[j].astype(f32)
        restored = split_dot(summed, signs) * (1.0 / math.sqrt(HB))
        value = (residual_ref[j].astype(f32) + restored).astype(out_ref.dtype)
        out_ref[j] = value
        turned_ref[j] = value.T


def update(own, terms, residual, signs):
    vmem = pl.BlockSpec(memory_space=pltpu.VMEM)
    blocks, tokens, _ = residual.shape
    return pl.pallas_call(
        update_kernel,
        in_specs=[vmem] * (len(terms) + 3),
        out_specs=[vmem, vmem],
        out_shape=[
            jax.ShapeDtypeStruct(residual.shape, residual.dtype),
            jax.ShapeDtypeStruct((blocks, HB, tokens), residual.dtype),
        ],
        compiler_params=pltpu.CompilerParams(vmem_limit_bytes=24 << 20),
        name="update",
    )(own, *terms, residual, signs)


def query_kernel(info, units, *refs):
    count, chunk, first, last, following = (info[n] for n in ("count", "chunk", "first", "last", "following"))
    refs = list(refs)
    streams = [refs.pop(0) for _ in range(count)]
    gain_ref = refs.pop(0)
    now = [refs.pop(0) for _ in range(count)]
    if not last:
        weight_ref = refs.pop(0)
    if not first:
        acc_in, square_in = refs.pop(0), refs.pop(0)
    if last:
        cos_ref, sin_ref, out_ref = refs
    else:
        acc_ref, square_ref, *ahead, sems = refs
        coming = next_fetches(weight_ref, units, range(count, count + following), ahead, sems)
        for copy in coming:
            copy.start()
    blocks, _, tokens = streams[0].shape
    width = blocks * HB
    chunks = now[0].shape[0] // chunk
    squares = None if first else square_in[...]
    factors = []
    for k in range(count):
        parts = []
        gains = gain_ref[pl.ds(pl.multiple_of(units[k] * blocks, blocks), blocks), :].T
        for j in range(blocks):
            value = streams[k][j].astype(f32)
            squares = value * value if squares is None else squares + value * value
            parts.append((value * gains[:, j : j + 1]).astype(bf16))
        factors.append(jnp.concatenate(parts, axis=0))
    if last:
        mean_square = jnp.sum(squares, axis=0, keepdims=True) * (1.0 / info["width"])
        root = lax.rsqrt(mean_square + eps_norm)
        even = lax.broadcasted_iota(jnp.int32, (HEAD, tokens), 0) % 2 == 0
    else:
        square_ref[...] = squares
    for c in range(chunks):
        here = slice(c * chunk, (c + 1) * chunk)
        total = None if first else acc_in[here, :]
        for k in range(count):
            product = jnp.dot(now[k][here, :], factors[k], preferred_element_type=f32)
            total = product if total is None else total + product
        if not last:
            acc_ref[here, :] = total
            continue
        for h in range(chunk // HEAD):
            value = total[h * HEAD : (h + 1) * HEAD, :] * root
            other = jnp.where(even, pltpu.roll(value, HEAD - 1, 0), pltpu.roll(value, 1, 0))
            rotated = value * cos_ref[...] + other * sin_ref[...]
            out_ref[c * chunk + h * HEAD : c * chunk + (h + 1) * HEAD, :] = rotated.astype(out_ref.dtype)
    if not last:
        for copy in coming:
            copy.wait()


def query_units(streams, units, later, gain, query_weight, ahead, carried=None, tables=None):
    count, following = len(streams), len(later)
    blocks, _, tokens = streams[0].shape
    columns, width = query_weight.shape
    unit_width = blocks * HB
    first, last = carried is None, tables is not None
    info = dict(count=count, chunk=columns, first=first, last=last, following=following, width=width)
    vmem = pl.BlockSpec(memory_space=pltpu.VMEM)
    args = [jnp.stack([*units, *later]), *streams, gain, *ahead]
    in_specs = [pl.BlockSpec(memory_space=pltpu.SMEM)] + [vmem] * (2 * count + 1)
    if not last:
        args.append(query_weight)
        in_specs.append(pl.BlockSpec(memory_space=pltpu.HBM))
    rest = [*(carried or ()), *(tables or ())]
    if last:
        out_shape, scratch = [jax.ShapeDtypeStruct((columns, tokens), bf16)], []
    else:
        out_shape = [
            jax.ShapeDtypeStruct((columns, tokens), f32),
            jax.ShapeDtypeStruct((HB, tokens), f32),
        ]
        out_shape += [jax.ShapeDtypeStruct((columns, unit_width), bf16)] * following
        scratch = [pltpu.SemaphoreType.DMA((following,))]
    return pl.pallas_call(
        functools.partial(query_kernel, info),
        in_specs=in_specs + [vmem] * len(rest),
        out_specs=[vmem] * len(out_shape),
        out_shape=out_shape,
        scratch_shapes=scratch,
        compiler_params=pltpu.CompilerParams(vmem_limit_bytes=42 << 20),
        cost_estimate=pl.CostEstimate(
            flops=2 * tokens * columns * unit_width * count,
            bytes_accessed=2 * columns * unit_width * count,
            transcendentals=0,
        ),
        name="query_units",
    )(*args, *rest)


def rotary_tables(positions):
    row_ids = jnp.arange(HEAD, dtype=jnp.int32)
    inv_freq = jnp.exp((row_ids // 2).astype(f32) * (-2.0 * math.log(rope_base) / HEAD))
    angles = inv_freq[:, None] * positions[None, :]
    sign = jnp.where(row_ids % 2 == 0, -1.0, 1.0).astype(f32)
    return jnp.cos(angles), jnp.sin(angles) * sign[:, None]


def pairs_of(partner):
    found = []
    for z in range(4):
        for x in range(2):
            for core in range(2):
                pz, px, pcore = partner(z, x, core)
                found.append(((2 * z + x) * 2 + core, (2 * pz + px) * 2 + pcore))
    return found


ACROSS = pairs_of(lambda z, x, core: (z, 1 - x, core))
TWINS = pairs_of(lambda z, x, core: (z ^ 1, x, core))
MIDDLE = pairs_of(lambda z, x, core: (3 - z, x, core) if z in (1, 2) else (z, x, 1 - core))


def after(*values):
    return lax.optimization_barrier(values)


def send(value, pairs):
    return lax.ppermute(value.astype(bf16), ("tensor", "replica"), pairs)


def local_eight(hidden, down_weight, residual, norm_gain, query_weight, prefix_len, seg_lengths):
    place = lax.axis_index("tensor").astype(jnp.int32)
    z, x = place // 2, place % 2
    tokens = hidden.shape[2]
    slot = [z, z ^ 1, jnp.where(z < 2, 2, 1), jnp.where(z < 2, 3, 0)]
    mine = [2 * s + x for s in slot]
    theirs = [2 * s + 1 - x for s in slot]
    inner = (z == 1) | (z == 2)

    def down(units, dtypes, rows):
        return down_units(rows, down_weight, signs, units, dtypes)

    def only(here, value):
        return jnp.where(here, value, jnp.zeros_like(value))

    out3, rows, signs = down_units(hidden[0], down_weight, None, [theirs[3]], [bf16])
    got3 = send(out3, ACROSS)
    own3, out2 = down([mine[3], theirs[2]], [f32, bf16], rows)
    got2 = send(out2, ACROSS)
    part3, rows = after((own3 + got3).astype(bf16), rows)
    add3 = only(inner, send(part3, TWINS))
    own2, out1 = down([mine[2], theirs[1]], [f32, bf16], rows)
    got1 = send(out1, ACROSS)
    part2 = (own2 + got2).astype(bf16)
    add2 = only(inner, send(part2, TWINS))
    part3 = (own3 + got3 + add3).astype(bf16)
    part2, part3, rows = after(part2, part3, rows)
    add1 = only(inner, send(part3, MIDDLE))
    own1, out0 = down([mine[1], theirs[0]], [f32, bf16], rows)
    got0 = send(out0, ACROSS)
    part1 = (own1 + got1 + add1).astype(bf16)
    part2 = only(inner, (own2 + got2 + add2).astype(bf16))
    part1, part2, rows = after(part1, part2, rows)
    from1 = send(part1, TWINS)
    from2 = send(part2, MIDDLE)
    early = [mine[0], theirs[0]]
    own0, ahead0, held = down_units(rows, down_weight, signs, [mine[0]], [f32], query_weight, early)
    from2, got0, _ = after(from2, got0, from1)
    updated, unit0 = update(own0, [got0, from2, from1], residual[0], signs)

    gain = norm_gain.reshape(-1, HB)

    def query(streams, units, later, ahead, state=None):
        acc, square, *ahead = query_units(streams, units, later, gain, query_weight, ahead, state)
        return (acc, square), ahead

    side0 = send(unit0, ACROSS)
    unit1 = send(unit0, TWINS)
    inner2 = send(unit0, MIDDLE)
    state, ahead = query([unit0], [mine[0]], [mine[1]], [ahead0])
    unit1, state = after(unit1, state)
    inner2, _ = after(inner2, unit1)
    side1 = send(unit1, ACROSS)
    inner3 = send(unit1, MIDDLE)
    unit2 = jnp.where(inner, inner2, send(inner2, TWINS))
    state, ahead = query([side0, unit1], [theirs[0], mine[1]], [theirs[1], mine[2]], [held, *ahead], state)
    inner3, state = after(inner3, state)
    unit3 = jnp.where(inner, inner3, send(inner3, TWINS))
    side2 = send(unit2, ACROSS)
    state, ahead = query([side1, unit2], [theirs[1], mine[2]], [theirs[2], mine[3]], ahead, state)
    unit3, state = after(unit3, state)
    prefix, lengths, _ = after(prefix_len[0], seg_lengths[0], unit3)
    tables = rotary_tables(positions_of(prefix, lengths, tokens))
    side3 = send(unit3, ACROSS)
    state, ahead = query([side2, unit3], [theirs[2], mine[3]], [theirs[3]], ahead, state)
    query_one, = query_units([side3], [theirs[3]], [], gain, query_weight, ahead, state, tables)
    return (updated[None], query_one[None])


def solution(mesh):
    in_specs = (
        P(("groups", "replica"), "tensor", None),
        P("tensor", None),
        P(("groups", "replica"), "tensor", None, None),
        P(),
        P("tensor", None),
        P(("groups", "replica")),
        P(("groups", "replica"), None),
    )
    out_specs = (
        P(("groups", "replica"), "tensor", None, None),
        P(("groups", "replica"), "tensor", None),
    )
    local = local_eight if mesh.shape["tensor"] == 8 and mesh.shape["replica"] == 2 else local_general
    return jax.shard_map(local, mesh=mesh, in_specs=in_specs, out_specs=out_specs, check_vma=False)
```

```python
import functools
import math

import jax
import jax.numpy as jnp
from jax import lax
from jax.experimental import pallas as pl
from jax.experimental.pallas import tpu as pltpu
from jax.sharding import PartitionSpec as P

HEAD = 128
HB = 128


eps_norm = 1e-05
eps_scale = 1e-06
code_top = 448.0
least_normal = 0.015625
rope_base = 500000.0

bf16 = jnp.bfloat16
f32 = jnp.float32


def hadamard_table(order_size):
    row_ids = lax.broadcasted_iota(jnp.int32, (order_size, order_size), 0)
    col_ids = lax.broadcasted_iota(jnp.int32, (order_size, order_size), 1)
    common = jnp.bitwise_and(row_ids, col_ids)
    parity = jnp.zeros((order_size, order_size), jnp.int32)
    for shift_bits in range(order_size.bit_length()):
        parity = parity + jnp.bitwise_and(jnp.right_shift(common, shift_bits), 1)
    sign_table = (1 - 2 * (parity % 2)).astype(jnp.float32)
    return sign_table / math.sqrt(order_size)


def hadamard_signs():
    row_ids = lax.broadcasted_iota(jnp.int32, (2 * HB, HB), 0)
    col_ids = lax.broadcasted_iota(jnp.int32, (2 * HB, HB), 1)
    common = jnp.bitwise_and(row_ids, col_ids)
    for shift_bits in (4, 2, 1):
        common = jnp.bitwise_xor(common, jnp.right_shift(common, shift_bits))
    return (1 - 2 * jnp.bitwise_and(common, 1)).astype(f32).astype(bf16)


def grid_code(scaled):
    magnitude = jnp.maximum(jnp.abs(scaled), least_normal)
    binade = jnp.floor(jnp.log2(magnitude))
    spacing = jnp.exp2(binade - 3.0)
    return spacing * jnp.floor(scaled / spacing + 0.5)


def positions_of(prefix_one, length_row, token_count):
    seg_total = length_row.shape[0]
    before = lax.broadcasted_iota(jnp.int32, (seg_total, seg_total), 0) < lax.broadcasted_iota(
        jnp.int32, (seg_total, seg_total), 1
    )
    seg_starts = jnp.sum(jnp.where(before, length_row[:, None], 0), axis=0)
    token_place = lax.broadcasted_iota(jnp.int32, (token_count, seg_total), 0)
    started = token_place >= seg_starts[None, :]
    seg_start = jnp.max(jnp.where(started, seg_starts[None, :], 0), axis=1)
    return (prefix_one + token_place[:, 0] - seg_start).astype(jnp.float32)


def rotate_rows(projected, columns, positions):
    token_count = projected.shape[1]
    even_columns = columns.reshape(-1, 2)[:, 0]
    pair_index = even_columns % HEAD // 2
    inv_freq = jnp.exp(pair_index.astype(jnp.float32) * (-2.0 * math.log(rope_base) / HEAD))
    angles = inv_freq[:, None] * positions[None, :]
    cosine = jnp.cos(angles)
    sine_part = jnp.sin(angles)
    paired = projected.reshape(-1, 2, token_count)
    even_part = paired[:, 0]
    odd_part = paired[:, 1]
    rotated_pairs = jnp.stack(
        [even_part * cosine - odd_part * sine_part, even_part * sine_part + odd_part * cosine],
        axis=1,
    )
    return rotated_pairs.reshape(projected.shape)


def local_general(hidden, down_weight, residual, norm_gain, query_weight, prefix_len, seg_lengths):
    members = lax.axis_size("tensor")
    span_len = hidden.shape[2]
    model_width = down_weight.shape[1]
    blocks = model_width // HB
    splits = max(1, members // blocks)
    piece_len = span_len // splits
    item_total = splits * blocks
    per_device = item_total // members
    hadamard = hadamard_table(HB)
    partial_value = lax.dot_general(
        hidden[0], down_weight, (((0,), (0,)), ((), ())), preferred_element_type=jnp.float32
    )
    partial_value = partial_value.reshape(splits, piece_len, blocks, HB).transpose(0, 2, 1, 3)
    rotated = jnp.einsum("sbch,hk->sbck", partial_value, hadamard, precision=lax.Precision.HIGHEST)
    block_scale = (jnp.max(jnp.abs(rotated), axis=3, keepdims=True) + eps_scale) / code_top
    block_code = grid_code(rotated / block_scale).astype(jnp.bfloat16)
    sent_codes = block_code.reshape(members, per_device, piece_len, HB)
    sent_scales = block_scale.reshape(members, per_device, piece_len)
    got_codes = lax.all_to_all(sent_codes, "tensor", split_axis=0, concat_axis=0, tiled=True)
    got_scales = lax.all_to_all(
        sent_scales.astype(jnp.bfloat16), "tensor", split_axis=0, concat_axis=0, tiled=True
    ).astype(sent_scales.dtype)
    running = jnp.sum(got_codes.astype(jnp.float32) * got_scales[..., None], axis=0)
    item_count = running.shape[0]
    unrotated = jnp.dot(running.reshape(-1, HB), hadamard, precision=lax.Precision.HIGHEST)
    restored = unrotated.reshape(item_count, piece_len, HB)
    updated = (residual[0].astype(jnp.float32) + restored).astype(jnp.bfloat16)
    gathered = lax.all_gather(updated, "tensor", axis=0, tiled=True)
    widened = gathered.astype(jnp.float32).reshape(splits, blocks, piece_len, HB)
    mean_square = jnp.mean(widened * widened, axis=(1, 3), keepdims=True)
    gain_blocks = norm_gain.reshape(1, blocks, 1, HB)
    normed = (widened * lax.rsqrt(mean_square + eps_norm) * gain_blocks).astype(jnp.bfloat16)
    column_count = query_weight.shape[0]
    weight_blocks = query_weight.reshape(column_count, blocks, HB)
    projected = jnp.einsum(
        "qbh,sbch->qsc", weight_blocks, normed, preferred_element_type=jnp.float32
    ).reshape(column_count, span_len)
    positions = positions_of(prefix_len[0], seg_lengths[0], span_len)
    columns = lax.axis_index("tensor") * column_count + lax.iota(jnp.int32, column_count)
    query_one = rotate_rows(projected, columns, positions).astype(jnp.bfloat16)
    return (updated[None], query_one[None])


def split_dot(value, signs):
    high = value.astype(bf16)
    low = (value - high.astype(f32)).astype(bf16)
    return jnp.dot(jnp.concatenate([high, low], axis=1), signs, preferred_element_type=f32)


def coded(total, signs):
    for j in range(total.shape[1] // HB):
        rotated = split_dot(total[:, j * HB : (j + 1) * HB], signs)
        top = jnp.max(jnp.abs(rotated), axis=1, keepdims=True) * (1.0 / math.sqrt(HB)) + eps_scale
        scaled = rotated * ((code_top / math.sqrt(HB)) / top)
        anchor = jnp.maximum(jnp.abs(scaled), least_normal) * (2.0**20 - 4.0)
        code = (scaled + anchor) - anchor
        yield code * (top * (1.0 / code_top))


def next_fetches(weight_ref, units, places, outs, sems):
    width = outs[0].shape[1]
    return [
        pltpu.make_async_copy(
            weight_ref.at[:, pl.ds(pl.multiple_of(units[p] * width, width), width)], out, sems.at[k]
        )
        for k, (p, out) in enumerate(zip(places, outs))
    ]


def down_kernel(count, first, later, chunk, units, *refs):
    if later:
        query_ref, *refs, held, sems, ahead_sems = refs
        ahead = refs[-later:]
        refs = [*refs[:-later], held, sems]
    if first:
        rows_ref, weight_ref, out, turned, signs_out, held, sems, held_rows, row_sem = refs
        outs = [out]
    else:
        rows_ref, weight_ref, signs_ref, *outs, held, sems = refs
    depth, width = held.shape[1:]
    chunks = depth // chunk

    def fetch(k, c):
        here = pl.ds(c * chunk, chunk)
        columns = pl.ds(pl.multiple_of(units[k] * width, width), width)
        return pltpu.make_async_copy(weight_ref.at[here, columns], held.at[k, here], sems.at[k, c])

    if first:
        bring = pltpu.make_async_copy(rows_ref, held_rows, row_sem)
        bring.start()
    for k in range(count):
        for c in range(chunks):
            fetch(k, c).start()
    coming = next_fetches(query_ref, units, range(count, count + later), ahead, ahead_sems) if later else []
    for copy in coming:
        copy.start()
    if first:
        signs = hadamard_signs()
        signs_out[...] = signs
        bring.wait()
    else:
        signs = signs_ref[...]
    for k in range(count):
        total = None
        for c in range(chunks):
            here = slice(c * chunk, (c + 1) * chunk)
            if first:
                rows = held_rows[here, :].T
                turned[:, here] = rows
            else:
                rows = rows_ref[:, here]
            fetch(k, c).wait()
            product = jnp.dot(rows, held[k, here, :], preferred_element_type=f32)
            total = product if total is None else total + product
        for j, value in enumerate(coded(total, signs)):
            outs[k][j] = value.astype(outs[k].dtype)
    for copy in coming:
        copy.wait()


def down_units(rows, down_weight, signs, units, dtypes, query_weight=None, later=()):
    count = len(dtypes)
    first = signs is None
    tokens, depth = rows.shape[::-1] if first else rows.shape
    unit_width = down_weight.shape[1] // 8
    chunk = 512 if depth % 512 == 0 else depth
    vmem = pl.BlockSpec(memory_space=pltpu.VMEM)
    hbm = pl.BlockSpec(memory_space=pltpu.HBM)
    out_shape = [jax.ShapeDtypeStruct((unit_width // HB, tokens, HB), d) for d in dtypes]
    scratch = [
        pltpu.VMEM((count, depth, unit_width), bf16),
        pltpu.SemaphoreType.DMA((count, depth // chunk)),
    ]
    if first:
        out_shape.append(jax.ShapeDtypeStruct((tokens, depth), bf16))
        out_shape.append(jax.ShapeDtypeStruct((2 * HB, HB), bf16))
        scratch += [pltpu.VMEM((depth, tokens), bf16), pltpu.SemaphoreType.DMA]
        args, in_specs = (rows, down_weight), [hbm, hbm]
    else:
        args, in_specs = (rows, down_weight, signs), [vmem, hbm, vmem]
    if later:
        args, in_specs = (query_weight, *args), [hbm, *in_specs]
        units = [*units, *later]
        out_shape += [jax.ShapeDtypeStruct((query_weight.shape[0], unit_width), bf16)] * len(later)
        scratch.append(pltpu.SemaphoreType.DMA((len(later),)))
    return pl.pallas_call(
        functools.partial(down_kernel, count, first, len(later), chunk),
        in_specs=[pl.BlockSpec(memory_space=pltpu.SMEM), *in_specs],
        out_specs=[vmem] * len(out_shape),
        out_shape=out_shape,
        scratch_shapes=scratch,
        compiler_params=pltpu.CompilerParams(vmem_limit_bytes=(48 if first or later else 32) << 20),
        cost_estimate=pl.CostEstimate(
            flops=2 * tokens * depth * unit_width * count,
            bytes_accessed=2 * depth * unit_width * count,
            transcendentals=0,
        ),
        name="down_units",
    )(jnp.stack(units), *args)


def update_kernel(own_ref, *refs):
    *terms, residual_ref, signs_ref, out_ref, turned_ref = refs
    signs = signs_ref[...]
    for j in range(own_ref.shape[0]):
        summed = own_ref[j]
        for term in terms:
            summed = summed + term[j].astype(f32)
        restored = split_dot(summed, signs) * (1.0 / math.sqrt(HB))
        value = (residual_ref[j].astype(f32) + restored).astype(out_ref.dtype)
        out_ref[j] = value
        turned_ref[j] = value.T


def update(own, terms, residual, signs):
    vmem = pl.BlockSpec(memory_space=pltpu.VMEM)
    blocks, tokens, _ = residual.shape
    return pl.pallas_call(
        update_kernel,
        in_specs=[vmem] * (len(terms) + 3),
        out_specs=[vmem, vmem],
        out_shape=[
            jax.ShapeDtypeStruct(residual.shape, residual.dtype),
            jax.ShapeDtypeStruct((blocks, HB, tokens), residual.dtype),
        ],
        compiler_params=pltpu.CompilerParams(vmem_limit_bytes=24 << 20),
        name="update",
    )(own, *terms, residual, signs)


def query_kernel(info, units, *refs):
    count, chunk, first, last, following = (info[n] for n in ("count", "chunk", "first", "last", "following"))
    refs = list(refs)
    streams = [refs.pop(0) for _ in range(count)]
    gain_ref = refs.pop(0)
    now = [refs.pop(0) for _ in range(count)]
    if not last:
        weight_ref = refs.pop(0)
    if not first:
        acc_in, square_in = refs.pop(0), refs.pop(0)
    if last:
        cos_ref, sin_ref, out_ref = refs
    else:
        acc_ref, square_ref, *ahead, sems = refs
        coming = next_fetches(weight_ref, units, range(count, count + following), ahead, sems)
        for copy in coming:
            copy.start()
    blocks, _, tokens = streams[0].shape
    width = blocks * HB
    chunks = now[0].shape[0] // chunk
    squares = None if first else square_in[...]
    factors = []
    for k in range(count):
        parts = []
        gains = gain_ref[pl.ds(pl.multiple_of(units[k] * blocks, blocks), blocks), :].T
        for j in range(blocks):
            value = streams[k][j].astype(f32)
            squares = value * value if squares is None else squares + value * value
            parts.append((value * gains[:, j : j + 1]).astype(bf16))
        factors.append(jnp.concatenate(parts, axis=0))
    if last:
        mean_square = jnp.sum(squares, axis=0, keepdims=True) * (1.0 / info["width"])
        root = lax.rsqrt(mean_square + eps_norm)
        even = lax.broadcasted_iota(jnp.int32, (HEAD, tokens), 0) % 2 == 0
    else:
        square_ref[...] = squares
    for c in range(chunks):
        here = slice(c * chunk, (c + 1) * chunk)
        total = None if first else acc_in[here, :]
        for k in range(count):
            product = jnp.dot(now[k][here, :], factors[k], preferred_element_type=f32)
            total = product if total is None else total + product
        if not last:
            acc_ref[here, :] = total
            continue
        for h in range(chunk // HEAD):
            value = total[h * HEAD : (h + 1) * HEAD, :] * root
            other = jnp.where(even, pltpu.roll(value, HEAD - 1, 0), pltpu.roll(value, 1, 0))
            rotated = value * cos_ref[...] + other * sin_ref[...]
            out_ref[c * chunk + h * HEAD : c * chunk + (h + 1) * HEAD, :] = rotated.astype(out_ref.dtype)
    if not last:
        for copy in coming:
            copy.wait()


def query_units(streams, units, later, gain, query_weight, ahead, carried=None, tables=None):
    count, following = len(streams), len(later)
    blocks, _, tokens = streams[0].shape
    columns, width = query_weight.shape
    unit_width = blocks * HB
    first, last = carried is None, tables is not None
    info = dict(count=count, chunk=columns, first=first, last=last, following=following, width=width)
    vmem = pl.BlockSpec(memory_space=pltpu.VMEM)
    args = [jnp.stack([*units, *later]), *streams, gain, *ahead]
    in_specs = [pl.BlockSpec(memory_space=pltpu.SMEM)] + [vmem] * (2 * count + 1)
    if not last:
        args.append(query_weight)
        in_specs.append(pl.BlockSpec(memory_space=pltpu.HBM))
    rest = [*(carried or ()), *(tables or ())]
    if last:
        out_shape, scratch = [jax.ShapeDtypeStruct((columns, tokens), bf16)], []
    else:
        out_shape = [
            jax.ShapeDtypeStruct((columns, tokens), f32),
            jax.ShapeDtypeStruct((HB, tokens), f32),
        ]
        out_shape += [jax.ShapeDtypeStruct((columns, unit_width), bf16)] * following
        scratch = [pltpu.SemaphoreType.DMA((following,))]
    return pl.pallas_call(
        functools.partial(query_kernel, info),
        in_specs=in_specs + [vmem] * len(rest),
        out_specs=[vmem] * len(out_shape),
        out_shape=out_shape,
        scratch_shapes=scratch,
        compiler_params=pltpu.CompilerParams(vmem_limit_bytes=42 << 20),
        cost_estimate=pl.CostEstimate(
            flops=2 * tokens * columns * unit_width * count,
            bytes_accessed=2 * columns * unit_width * count,
            transcendentals=0,
        ),
        name="query_units",
    )(*args, *rest)


def rotary_tables(positions):
    row_ids = jnp.arange(HEAD, dtype=jnp.int32)
    inv_freq = jnp.exp((row_ids // 2).astype(f32) * (-2.0 * math.log(rope_base) / HEAD))
    angles = inv_freq[:, None] * positions[None, :]
    sign = jnp.where(row_ids % 2 == 0, -1.0, 1.0).astype(f32)
    return jnp.cos(angles), jnp.sin(angles) * sign[:, None]


def pairs_of(partner):
    found = []
    for z in range(4):
        for x in range(2):
            for core in range(2):
                pz, px, pcore = partner(z, x, core)
                found.append(((2 * z + x) * 2 + core, (2 * pz + px) * 2 + pcore))
    return found


ACROSS = pairs_of(lambda z, x, core: (z, 1 - x, core))
TWINS = pairs_of(lambda z, x, core: (z ^ 1, x, core))
MIDDLE = pairs_of(lambda z, x, core: (3 - z, x, core) if z in (1, 2) else (z, x, 1 - core))


def after(*values):
    return lax.optimization_barrier(values)


def send(value, pairs):
    return lax.ppermute(value.astype(bf16), ("tensor", "replica"), pairs)


def local_eight(hidden, down_weight, residual, norm_gain, query_weight, prefix_len, seg_lengths):
    place = lax.axis_index("tensor").astype(jnp.int32)
    z, x = place // 2, place % 2
    tokens = hidden.shape[2]
    slot = [z, z ^ 1, jnp.where(z < 2, 2, 1), jnp.where(z < 2, 3, 0)]
    mine = [2 * s + x for s in slot]
    theirs = [2 * s + 1 - x for s in slot]
    inner = (z == 1) | (z == 2)

    def down(units, dtypes, rows):
        return down_units(rows, down_weight, signs, units, dtypes)

    def only(here, value):
        return jnp.where(here, value, jnp.zeros_like(value))

    out3, rows, signs = down_units(hidden[0], down_weight, None, [theirs[3]], [bf16])
    got3 = send(out3, ACROSS)
    own3, out2 = down([mine[3], theirs[2]], [f32, bf16], rows)
    got2 = send(out2, ACROSS)
    part3, rows = after((own3 + got3).astype(bf16), rows)
    add3 = only(inner, send(part3, TWINS))
    own2, out1 = down([mine[2], theirs[1]], [f32, bf16], rows)
    got1 = send(out1, ACROSS)
    part2 = (own2 + got2).astype(bf16)
    add2 = only(inner, send(part2, TWINS))
    part3 = (own3 + got3 + add3).astype(bf16)
    part2, part3, rows = after(part2, part3, rows)
    add1 = only(inner, send(part3, MIDDLE))
    own1, out0 = down([mine[1], theirs[0]], [f32, bf16], rows)
    got0 = send(out0, ACROSS)
    part1 = (own1 + got1 + add1).astype(bf16)
    part2 = only(inner, (own2 + got2 + add2).astype(bf16))
    part1, part2, rows = after(part1, part2, rows)
    from1 = send(part1, TWINS)
    from2 = send(part2, MIDDLE)
    early = [mine[0], theirs[0]]
    own0, ahead0, held = down_units(rows, down_weight, signs, [mine[0]], [f32], query_weight, early)
    from2, got0, _ = after(from2, got0, from1)
    updated, unit0 = update(own0, [got0, from2, from1], residual[0], signs)

    gain = norm_gain.reshape(-1, HB)

    def query(streams, units, later, ahead, state=None):
        acc, square, *ahead = query_units(streams, units, later, gain, query_weight, ahead, state)
        return (acc, square), ahead

    side0 = send(unit0, ACROSS)
    unit1 = send(unit0, TWINS)
    inner2 = send(unit0, MIDDLE)
    state, ahead = query([unit0], [mine[0]], [mine[1]], [ahead0])
    unit1, state = after(unit1, state)
    inner2, _ = after(inner2, unit1)
    side1 = send(unit1, ACROSS)
    inner3 = send(unit1, MIDDLE)
    unit2 = jnp.where(inner, inner2, send(inner2, TWINS))
    state, ahead = query([side0, unit1], [theirs[0], mine[1]], [theirs[1], mine[2]], [held, *ahead], state)
    inner3, state = after(inner3, state)
    unit3 = jnp.where(inner, inner3, send(inner3, TWINS))
    side2 = send(unit2, ACROSS)
    now, kept = ahead
    state, ahead = query([side1], [theirs[1]], [theirs[2], mine[3]], [now], state)
    unit3, state = after(unit3, state)
    prefix, lengths, _ = after(prefix_len[0], seg_lengths[0], unit3)
    tables = rotary_tables(positions_of(prefix, lengths, tokens))
    side3 = send(unit3, ACROSS)
    state, ahead = query([unit2, side2, unit3], [mine[2], theirs[2], mine[3]], [theirs[3]], [kept, *ahead], state)
    query_one, = query_units([side3], [theirs[3]], [], gain, query_weight, ahead, state, tables)
    return (updated[None], query_one[None])


def solution(mesh):
    in_specs = (
        P(("groups", "replica"), "tensor", None),
        P("tensor", None),
        P(("groups", "replica"), "tensor", None, None),
        P(),
        P("tensor", None),
        P(("groups", "replica")),
        P(("groups", "replica"), None),
    )
    out_specs = (
        P(("groups", "replica"), "tensor", None, None),
        P(("groups", "replica"), "tensor", None),
    )
    local = local_eight if mesh.shape["tensor"] == 8 and mesh.shape["replica"] == 2 else local_general
    return jax.shard_map(local, mesh=mesh, in_specs=in_specs, out_specs=out_specs, check_vma=False)
```
